32 devices in a mesh: groups: 2 (over y), adapter: 4 (over z), tensor: 4 (over x, core).
Axes of the slice: x: 2, y: 2, z: 4, core: 2. Of those that a mesh axis runs over, the one named last changes fastest.
Arguments:
- queries: bfloat16 [256, 8192], P(('groups', 'adapter'), 'tensor'), parts along dimension 0, may hold values from -11 to 11
- cache_keys: bfloat16 [256, 64, 1024], P(('groups', 'adapter'), None, 'tensor'), parts along dimension 0, may hold values from -11 to 11
- cached_value_rows: bfloat16 [256, 64, 1024], P(('groups', 'adapter'), None, 'tensor'), parts along dimension 0, may hold values from -6 to 6
- new_keys: bfloat16 [256, 1024], P(('groups', 'adapter'), 'tensor'), parts along dimension 0, may hold values from -11 to 11
- fresh_value_rows: bfloat16 [256, 1024], P(('groups', 'adapter'), 'tensor'), parts along dimension 0, may hold values from -6 to 6
- lengths: int32 [256], P(('groups', 'adapter')), parts along dimension 0, may hold values from 1 to 64, as said below
- adapter_ids: int32 [256], P('groups'), parts along dimension 0, may hold values from 0 to 7, as said below
- adapter_slots: int32 [8], replicated, may hold values from 0 to 7, each once
- out_weight: bfloat16 [8192, 8192], P('tensor', 'adapter'), may hold values from -0.0625 to 0.0625
- shrink_weight: bfloat16 [8, 8192, 64], P('adapter', 'tensor'), may hold values from -0.0625 to 0.0625
- expand_weight: bfloat16 [8, 64, 8192], P('adapter', 'tensor'), may hold values from -0.75 to 0.75
Outputs:
- mixed: bfloat16 [256, 8192], P('groups', 'adapter'), parts along dimension 0
The draws below stay inside these ranges and needn't reach their ends.
There are 2 independent parts, one for each index of `groups`. The reference program is written for one: setup_inputs(seed, part) draws one part's arguments, and reference() takes and returns one part's arrays. A program takes and returns all parts, laid end to end along the dimension named above; an argument that names none is the same for every part. Nothing has to cross between parts.
Inputs may be any that keep to these rules, and one draw needn't show every extreme that they name: `adapter_ids`: within each part, at most 32 requests name one adapter, and some adapter is named by exactly 32 requests. `lengths`: some request has length 64.
All inputs are finite; a program needn't handle non-finite values.
Results may differ from the reference program's by a relative error of at most 0.0085.
Values may be sent and summed in bfloat16 or wider, within the bound.
No kernel may reach another device: no remote copies, remote signals or barrier semaphores. Data moves between devices by JAX's collectives and lax.ppermute only.
A program may use at most 64 MiB of HBM per device.

```python
import math
import jax
import jax.numpy as jnp
from jax import lax

D = 8192
QUERY_HEADS = 64
KEY_VALUE_HEADS = 8
HEAD_SIZE = 128
RANK = 64
REQ = 32
CACHE_SLOTS_HELD = 64
TOKEN_COUNT = 128
ADAPTERS = 8
SLOTS = 32


def draw_queries(key, part):
    key = jax.random.fold_in(key, 21)
    drawn_output = jnp.clip(jax.random.normal(key, (TOKEN_COUNT, QUERY_HEADS * HEAD_SIZE), jnp.float32), -4.0, 4.0)
    return drawn_output.astype(jnp.bfloat16)


def draw_cache_keys(key, part):
    key = jax.random.fold_in(key, 22)
    drawn_output = jnp.clip(jax.random.normal(key, (TOKEN_COUNT, CACHE_SLOTS_HELD, KEY_VALUE_HEADS * HEAD_SIZE), jnp.float32), -4.0, 4.0)
    return drawn_output.astype(jnp.bfloat16)


def draw_new_keys(key, part):
    key = jax.random.fold_in(key, 23)
    drawn_output = jnp.clip(jax.random.normal(key, (TOKEN_COUNT, KEY_VALUE_HEADS * HEAD_SIZE), jnp.float32), -4.0, 4.0)
    return drawn_output.astype(jnp.bfloat16)


def draw_lengths(key, part):
    key = jax.random.fold_in(key, 24)
    first_key, second_key = jax.random.split(key)
    drawn = jax.random.randint(first_key, (TOKEN_COUNT,), 1, CACHE_SLOTS_HELD + 1)
    longest = jax.random.randint(second_key, (), 0, TOKEN_COUNT)
    drawn = jnp.where(jnp.arange(TOKEN_COUNT) == longest, CACHE_SLOTS_HELD, drawn)
    return drawn.astype(jnp.int32)


def draw_adapter_ids(key, part):
    key = jax.random.fold_in(key, 25)
    first_key, second_key, third_key = jax.random.split(key, 3)
    busiest = jax.random.randint(first_key, (), 0, ADAPTERS)
    tickets = jax.random.permutation(second_key, (ADAPTERS - 1) * SLOTS)[:TOKEN_COUNT - SLOTS]
    others = tickets // SLOTS
    others = others + (others >= busiest).astype(jnp.int32)
    chosen = jnp.concatenate([jnp.full((SLOTS,), busiest, jnp.int32), others.astype(jnp.int32)])
    return jax.random.permutation(third_key, chosen).astype(jnp.int32)


def levels(own_key, shape, shards, low, high):
    loudness = 1.0
    for dim, parts in shards:
        draws = jax.random.uniform(jax.random.fold_in(jax.random.fold_in(own_key, 6), dim), (parts,), jnp.float32, low / len(shards), high / len(shards))
        loudness = loudness * jnp.repeat(jnp.exp(draws), shape[dim] // parts).reshape((-1,) + (1,) * (len(shape) - 1 - dim))
    return loudness


def normal_values(stream_key, dims, scale, reach, cuts=(), held_as=jnp.bfloat16):
    values = scale * jax.random.normal(stream_key, dims, jnp.float32)
    if cuts:
        values = values * levels(stream_key, dims, cuts, -0.22, 0.18)
    return jnp.clip(values, -reach, reach).astype(held_as)


def setup_inputs(seed: int = 0, part: int = 0) -> dict:
    seeds = jax.random.split(jax.random.key(seed), 12)
    part_splits = jax.random.split(jax.random.fold_in(seeds[11], part), 12)
    return {
        "queries": draw_queries(jax.random.fold_in(jax.random.fold_in(seeds[11], part), 71), part),
        "cache_keys": draw_cache_keys(jax.random.fold_in(jax.random.fold_in(seeds[11], part), 71), part),
        "cached_value_rows": normal_values(part_splits[2], (TOKEN_COUNT, CACHE_SLOTS_HELD, KEY_VALUE_HEADS * HEAD_SIZE), 1.0, 6.0, ((0, 4), (2, 4))),
        "new_keys": draw_new_keys(jax.random.fold_in(jax.random.fold_in(seeds[11], part), 71), part),
        "fresh_value_rows": normal_values(part_splits[4], (TOKEN_COUNT, KEY_VALUE_HEADS * HEAD_SIZE), 1.0, 6.0, ((0, 4), (1, 4))),
        "lengths": draw_lengths(jax.random.fold_in(jax.random.fold_in(seeds[11], part), 71), part),
        "adapter_ids": draw_adapter_ids(jax.random.fold_in(jax.random.fold_in(seeds[11], part), 71), part),
        "adapter_slots": jax.random.permutation(seeds[7], ADAPTERS).astype(jnp.int32),
        "out_weight": normal_values(seeds[8], (QUERY_HEADS * HEAD_SIZE, D), (QUERY_HEADS * HEAD_SIZE) ** -0.5, 0.0625, ((0, 4), (1, 4))),
        "shrink_weight": normal_values(seeds[9], (ADAPTERS, QUERY_HEADS * HEAD_SIZE, RANK), (QUERY_HEADS * HEAD_SIZE) ** -0.5, 0.0625, ((0, 4), (1, 4))),
        "expand_weight": normal_values(seeds[10], (ADAPTERS, RANK, D), RANK ** -0.5, 0.75, ((0, 4), (1, 4))),
    }


adapter_scale = 2.0

def attend(query_row_block, key_row_block, value_row_block, request_own_keys, request_own_values, length_rows):
    row_count = query_row_block.shape[0]
    group_size = QUERY_HEADS // KEY_VALUE_HEADS
    factor_term = 1.0 / math.sqrt(HEAD_SIZE)
    query_head_count = query_row_block.astype(jnp.float32).reshape(row_count, KEY_VALUE_HEADS, group_size, HEAD_SIZE)
    key_head_count = key_row_block.astype(jnp.float32).reshape(row_count, CACHE_SLOTS_HELD, KEY_VALUE_HEADS, HEAD_SIZE)
    value_head_count = value_row_block.astype(jnp.float32).reshape(row_count, CACHE_SLOTS_HELD, KEY_VALUE_HEADS, HEAD_SIZE)
    scores = jnp.einsum('rkgd,rckd->rkgc', query_head_count, key_head_count) * factor_term
    request_own_score = jnp.einsum('ivhz,ivz->ivh', query_head_count, request_own_keys.astype(jnp.float32).reshape(row_count, KEY_VALUE_HEADS, HEAD_SIZE)) * factor_term
    valid = jnp.arange(CACHE_SLOTS_HELD)[None, None, None, :] < length_rows[:, None, None, None]
    scores = jnp.where(valid, scores, -jnp.inf)
    row_top = jnp.maximum(lax.optimization_barrier(jnp.max(scores, axis=-1)), request_own_score)
    powers = jnp.exp(scores - row_top[..., None])
    own_power = jnp.exp(request_own_score - row_top)
    row_total = lax.optimization_barrier(jnp.sum(powers, axis=-1)) + own_power
    weights = (powers / row_total[..., None]).astype(jnp.bfloat16)
    request_own_weight = (own_power / row_total).astype(jnp.bfloat16)
    blended_values = jnp.einsum('rkgc,rckd->rkgd', weights.astype(jnp.float32), value_head_count)
    blended_values = blended_values + request_own_weight.astype(jnp.float32)[..., None] * request_own_values.astype(jnp.float32).reshape(row_count, KEY_VALUE_HEADS, 1, HEAD_SIZE)
    return blended_values.reshape(row_count, QUERY_HEADS * HEAD_SIZE).astype(jnp.bfloat16)

def reference(queries, cache_keys, cached_value_rows, new_keys, fresh_value_rows, lengths, adapter_ids, adapter_slots, out_weight, shrink_weight, expand_weight):
    stored = adapter_slots[adapter_ids].astype(jnp.int32)
    blocks = TOKEN_COUNT // REQ

    def split_rows(array):
        return array.reshape((blocks, REQ) + array.shape[1:])

    def one_block(inputs):
        query_row_block, key_row_block, value_row_block, request_own_keys, request_own_values, length_rows, stored_rows = inputs
        attended = attend(query_row_block, key_row_block, value_row_block, request_own_keys, request_own_values, length_rows)
        base = jnp.dot(attended, out_weight, preferred_element_type=jnp.float32)
        down_maps = shrink_weight[stored_rows].astype(jnp.float32)
        shrunk = jnp.einsum('rk,rkn->rn', attended.astype(jnp.float32), down_maps).astype(jnp.bfloat16)
        up_maps = expand_weight[stored_rows].astype(jnp.float32)
        delta = jnp.einsum('rn,rnc->rc', shrunk.astype(jnp.float32), up_maps)
        return (base + adapter_scale * delta).astype(jnp.bfloat16)
    pieces = (split_rows(queries), split_rows(cache_keys), split_rows(cached_value_rows), split_rows(new_keys), split_rows(fresh_value_rows), split_rows(lengths), split_rows(stored))
    mixed = lax.map(one_block, pieces)
    return mixed.reshape(TOKEN_COUNT, D)
```

```python
import math

import jax
import jax.numpy as jnp
from jax import lax
from jax.sharding import PartitionSpec as P

HEAD_SIZE = 128
SLOTS = 32
ADAPTER_SCALE = 2.0
BF = jnp.bfloat16
F32 = jnp.float32


def attend(queries, cache_keys, cached_value_rows, new_keys, fresh_value_rows, lengths):
    requests = queries.shape[0]
    positions = cache_keys.shape[1]
    kv_local = cache_keys.shape[2] // HEAD_SIZE
    heads_local = queries.shape[1] // HEAD_SIZE
    group_size = heads_local // kv_local
    factor_term = 1.0 / math.sqrt(HEAD_SIZE)
    q = queries.reshape(requests, kv_local, group_size, HEAD_SIZE)
    k = cache_keys.reshape(requests, positions, kv_local, HEAD_SIZE)
    v = cached_value_rows.reshape(requests, positions, kv_local, HEAD_SIZE)
    scores = jnp.einsum("rkgd,rckd->rkgc", q, k, preferred_element_type=F32) * factor_term
    own = (
        jnp.einsum(
            "ivhz,ivz->ivh",
            q,
            new_keys.reshape(requests, kv_local, HEAD_SIZE),
            preferred_element_type=F32,
        )
        * factor_term
    )
    valid = jnp.arange(positions)[None, None, None, :] < lengths[:, None, None, None]
    scores = jnp.where(valid, scores, -jnp.inf)
    row_top = jnp.maximum(jnp.max(scores, axis=-1), own)
    powers = jnp.exp(scores - row_top[..., None])
    own_power = jnp.exp(own - row_top)
    row_total = jnp.sum(powers, axis=-1) + own_power
    weights = (powers / row_total[..., None]).astype(BF)
    own_weight = (own_power / row_total).astype(BF)
    blended = jnp.einsum("rkgc,rckd->rkgd", weights, v, preferred_element_type=F32)
    blended = blended + own_weight.astype(F32)[..., None] * fresh_value_rows.reshape(
        requests, kv_local, 1, HEAD_SIZE
    ).astype(F32)
    return blended.reshape(requests, heads_local * HEAD_SIZE).astype(BF)


def make_shards(n_adapter, n_tensor):
    def swap(x, axis, n, k):
        return lax.ppermute(x, axis, [(i, i ^ k) for i in range(n)])

    def shards(
        queries,
        cache_keys,
        cached_value_rows,
        new_keys,
        fresh_value_rows,
        lengths,
        adapter_ids,
        adapter_slots,
        out_weight,
        shrink_weight,
        expand_weight,
    ):
        a = lax.axis_index("adapter")
        t = lax.axis_index("tensor")
        low = t % 2
        adapters = adapter_slots.shape[0]
        per_owner, rank_part, width = expand_weight.shape
        rank = shrink_weight.shape[2]
        columns = out_weight.shape[1]
        half = columns // 2
        requests = queries.shape[0]
        tokens = adapter_ids.shape[0]
        owned = per_owner * SLOTS

        up = expand_weight.reshape(per_owner, rank_part, n_adapter, 2, half)
        up_keep = lax.dynamic_index_in_dim(up, low, 3, keepdims=False)
        up_send = lax.dynamic_index_in_dim(up, 1 - low, 3, keepdims=False)
        up = jnp.concatenate([up_keep, swap(up_send, "tensor", n_tensor, 1)], axis=1)
        step = 2
        while step < n_tensor:
            up = jnp.concatenate([up, swap(up, "tensor", n_tensor, step)], axis=1)
            step *= 2
        up = up.reshape(per_owner * rank, n_adapter * half)

        attended = attend(
            queries, cache_keys, cached_value_rows, new_keys, fresh_value_rows, lengths
        )

        matches = adapter_ids[:, None] == jnp.arange(adapters, dtype=jnp.int32)[None, :]
        counts = matches.astype(jnp.int32)
        rank_within = jnp.sum(jnp.cumsum(counts, axis=0) * counts, axis=1) - 1
        stored = jnp.sum(counts * adapter_slots[None, :], axis=1)
        owner = stored // per_owner
        slot = (stored % per_owner) * SLOTS + rank_within

        blocks = [attended] + [swap(attended, "adapter", n_adapter, k) for k in range(1, n_adapter)]
        rows = jnp.zeros((tokens, queries.shape[1]), BF)
        for k, block in enumerate(blocks):
            rows = lax.dynamic_update_slice(rows, block, ((a ^ k) * requests, 0))

        parts = jnp.einsum("rd,adn->arn", rows, shrink_weight, preferred_element_type=F32)
        here = stored[None, :] - a * per_owner == jnp.arange(per_owner, dtype=jnp.int32)[:, None]
        shrunk = jnp.sum(jnp.where(here[:, :, None], parts, 0.0), axis=0)
        step = 1
        while step < n_tensor:
            shrunk = shrunk + swap(shrunk, "tensor", n_tensor, step)
            step *= 2
        shrunk = shrunk.astype(BF)

        base = jnp.dot(rows, out_weight, preferred_element_type=F32)
        base_keep = lax.dynamic_slice_in_dim(base, low * half, half, 1)
        base_send = lax.dynamic_slice_in_dim(base, (1 - low) * half, half, 1).astype(BF)
        base = (base_keep + swap(base_send, "tensor", n_tensor, 1).astype(F32)).astype(BF)
        total = base.astype(F32)
        step = 2
        while step < n_tensor:
            total = total + swap(total.astype(BF), "tensor", n_tensor, step).astype(F32)
            step *= 2

        positions = jnp.arange(rank, dtype=jnp.int32)
        source = ((positions // rank_part) ^ t) * rank_part + positions % rank_part
        reorder = (jnp.arange(rank, dtype=jnp.int32)[:, None] == source[None, :]).astype(BF)
        select = (
            (jnp.arange(owned, dtype=jnp.int32)[:, None] == slot[None, :]) & (owner[None, :] == a)
        ).astype(BF)
        held = jnp.dot(jnp.dot(select, shrunk).astype(BF), reorder).astype(BF)
        in_block = (
            jnp.arange(owned, dtype=jnp.int32)[:, None] // SLOTS
            == jnp.arange(per_owner, dtype=jnp.int32)[None, :]
        )
        wide = jnp.where(in_block[:, :, None], held[:, None, :], 0).reshape(owned, -1)
        terms = jnp.dot(wide.astype(BF), up, preferred_element_type=F32).astype(BF)
        received = []
        for k in range(n_adapter):
            piece = lax.dynamic_slice_in_dim(terms, (a ^ k) * half, half, 1)
            received.append(swap(piece, "adapter", n_adapter, k) if k else piece)
        received = jnp.concatenate(received, axis=0)
        place = (
            ((owner ^ a) * owned + slot)[:, None]
            == jnp.arange(n_adapter * owned, dtype=jnp.int32)[None, :]
        ).astype(BF)
        delta = jnp.dot(place, received, preferred_element_type=F32)
        mine = (total + ADAPTER_SCALE * delta).astype(BF)
        other = swap(mine, "tensor", n_tensor, 1)
        return jnp.where(
            low == 0,
            jnp.concatenate([mine, other], axis=1),
            jnp.concatenate([other, mine], axis=1),
        )

    return shards


def solution(mesh):
    in_specs = (
        P(("groups", "adapter"), "tensor"),
        P(("groups", "adapter"), None, "tensor"),
        P(("groups", "adapter"), None, "tensor"),
        P(("groups", "adapter"), "tensor"),
        P(("groups", "adapter"), "tensor"),
        P(("groups", "adapter")),
        P("groups"),
        P(),
        P("tensor", "adapter"),
        P("adapter", "tensor", None),
        P("adapter", "tensor", None),
    )
    out_specs = P("groups", "adapter")
    shards = make_shards(mesh.shape["adapter"], mesh.shape["tensor"])
    return jax.shard_map(shards, mesh=mesh, in_specs=in_specs, out_specs=out_specs, check_vma=False)
```

```python
import functools
import math

import jax
import jax.numpy as jnp
from jax import lax
from jax.experimental import pallas as pl
from jax.experimental.pallas import tpu as pltpu
from jax.sharding import PartitionSpec as P

HEAD_SIZE = 128
SLOTS = 32
ADAPTER_SCALE = 2.0
BF = jnp.bfloat16
F32 = jnp.float32
VMEM = pl.BlockSpec(memory_space=pltpu.VMEM)
SMEM = pl.BlockSpec(memory_space=pltpu.SMEM)
ANY = pl.BlockSpec(memory_space=pl.ANY)


def attend_kernel(
    chunk, length_ref, q_hbm, k_hbm, v_hbm, nk_hbm, nv_hbm, out_ref, q_ref, k_ref, v_ref, nk_ref, nv_ref, sems
):
    requests, positions, kv_width = k_ref.shape
    heads = q_ref.shape[1] // HEAD_SIZE
    kv_heads = kv_width // HEAD_SIZE
    group = heads // kv_heads
    factor = 1.0 / math.sqrt(HEAD_SIZE)
    extended = positions + chunk

    small = [
        pltpu.make_async_copy(source, target, sems.at[2, i])
        for i, (source, target) in enumerate(((q_hbm, q_ref), (nk_hbm, nk_ref), (nv_hbm, nv_ref)))
    ]
    parts = [pl.ds(first, chunk) for first in range(0, requests, chunk)]
    keys = [
        pltpu.make_async_copy(k_hbm.at[part], k_ref.at[part], sems.at[0, i])
        for i, part in enumerate(parts)
    ]
    values = [
        pltpu.make_async_copy(v_hbm.at[part], v_ref.at[part], sems.at[1, i])
        for i, part in enumerate(parts)
    ]
    for copy in small:
        copy.start()
    for key, value in zip(keys, values):
        key.start()
        value.start()

    row_group = lax.broadcasted_iota(jnp.int32, (heads, kv_width), 0) // group
    lane_group = lax.broadcasted_iota(jnp.int32, (heads, kv_width), 1) // HEAD_SIZE
    diagonal = row_group == lane_group
    place = lax.broadcasted_iota(jnp.int32, (heads, extended), 1)
    ones = jnp.ones((extended, HEAD_SIZE), BF)
    for copy in small:
        copy.wait()
    for c, first in enumerate(range(0, requests, chunk)):
        q = q_ref[first : first + chunk].reshape(chunk, heads, HEAD_SIZE)
        new_keys = nk_ref[first : first + chunk]
        new_values = nv_ref[first : first + chunk]
        keys[c].wait()
        scores = []
        for i in range(chunk):
            r = first + i
            wide = jnp.where(
                diagonal, jnp.concatenate([q[i]] * kv_heads, axis=1), jnp.zeros((), BF)
            )
            score = lax.dot_general(
                wide,
                jnp.concatenate([k_ref[r], new_keys], axis=0),
                (((1,), (1,)), ((), ())),
                preferred_element_type=F32,
            )
            valid = (place < length_ref[r]) | (place == positions + i)
            scores.append(jnp.where(valid, score * factor, -jnp.inf))
        scores = jnp.stack(scores).reshape(chunk * heads, extended)
        powers = jnp.exp(scores - jnp.max(scores, axis=1, keepdims=True)).astype(BF)
        inverse = 1.0 / jnp.dot(powers, ones, preferred_element_type=F32)
        values[c].wait()
        outs = []
        for i in range(chunk):
            rows = slice(i * heads, (i + 1) * heads)
            blend = jnp.dot(
                powers[rows],
                jnp.concatenate([v_ref[first + i], new_values], axis=0),
                preferred_element_type=F32,
            )
            blend = jnp.concatenate(
                [
                    blend[g * group : (g + 1) * group, g * HEAD_SIZE : (g + 1) * HEAD_SIZE]
                    for g in range(kv_heads)
                ],
                axis=0,
            )
            outs.append((blend * inverse[rows]).astype(BF))
        out_ref[first : first + chunk] = jnp.stack(outs).reshape(chunk, heads * HEAD_SIZE)


def attend(queries, cache_keys, cached_value_rows, new_keys, fresh_value_rows, lengths):
    requests = queries.shape[0]
    chunk = 16 if requests % 16 == 0 else requests
    moved = (queries, cache_keys, cached_value_rows, new_keys, fresh_value_rows)
    return pl.pallas_call(
        functools.partial(attend_kernel, chunk),
        out_shape=jax.ShapeDtypeStruct(queries.shape, BF),
        in_specs=[SMEM] + [ANY] * 5,
        out_specs=VMEM,
        scratch_shapes=[pltpu.VMEM(x.shape, BF) for x in moved]
        + [pltpu.SemaphoreType.DMA((3, max(3, requests // chunk)))],
        compiler_params=pltpu.CompilerParams(vmem_limit_bytes=60 << 20),
        cost_estimate=pl.CostEstimate(
            flops=8 * queries.size * cache_keys.shape[1],
            bytes_accessed=4 * cache_keys.size,
            transcendentals=queries.size,
        ),
        name="attend",
    )(lengths, *moved)


def split_kernel(up_hbm, low_ref, high_ref, sems):
    half = low_ref.shape[3]
    low = lax.rem(lax.axis_index("tensor"), 2)
    copies = []
    for b in range(low_ref.shape[0]):
        for i, (ref, part) in enumerate(((low_ref, low), (high_ref, 1 - low))):
            start = pl.multiple_of((2 * b + part) * half, half)
            copies.append(
                pltpu.make_async_copy(up_hbm.at[:, :, pl.ds(start, half)], ref.at[b], sems.at[b, i])
            )
    for copy in copies:
        copy.start()
    for copy in copies:
        copy.wait()


def blockwise(position, count, size, index):
    moved = jnp.zeros_like(position)
    for k in range(count):
        inside = (position >= k * size) & (position < (k + 1) * size)
        moved = jnp.where(inside, position + ((index ^ k) - k) * size, moved)
    return moved


def ids_kernel(n_adapter, n_tensor, ids_ref, slots_ref, here_ref, select_ref, place_ref, order_ref):
    tokens, per_owner = here_ref.shape
    owned = select_ref.shape[0]
    rank = order_ref.shape[0]
    a = lax.axis_index("adapter")
    t = lax.axis_index("tensor")
    down = lax.broadcasted_iota(jnp.int32, (tokens, tokens), 0)
    across = lax.broadcasted_iota(jnp.int32, (tokens, tokens), 1)
    ids_row = ids_ref[...].astype(F32)
    ids_column = jnp.sum(jnp.where(down == across, ids_row, 0.0), axis=1, keepdims=True)
    same = ids_row == ids_column

    def stored(ids):
        return sum(
            jnp.where(ids == j, slots_ref[j].astype(F32), 0.0) for j in range(slots_ref.shape[0])
        )

    earlier = jnp.where(same & (across < down), 1.0, 0.0)
    stored_column = stored(ids_column)
    key_column = stored_column * SLOTS + jnp.sum(earlier, axis=1, keepdims=True)
    earlier = jnp.where(same & (down < across), 1.0, 0.0)
    key_row = stored(ids_row) * SLOTS + jnp.sum(earlier, axis=0, keepdims=True)
    key_column, key_row = key_column.astype(jnp.int32), key_row.astype(jnp.int32)
    adapter = lax.broadcasted_iota(jnp.int32, here_ref.shape, 1) + a * per_owner
    here_ref[...] = jnp.where(adapter == stored_column.astype(jnp.int32), 1.0, 0.0)
    slot = lax.broadcasted_iota(jnp.int32, select_ref.shape, 0) + a * owned
    select_ref[...] = jnp.where(slot == key_row, 1.0, 0.0).astype(BF)
    slot = lax.broadcasted_iota(jnp.int32, place_ref.shape, 1)
    slot = blockwise(slot, n_adapter, owned, a)
    place_ref[...] = jnp.where(slot == key_column, 1.0, 0.0).astype(BF)
    source = lax.broadcasted_iota(jnp.int32, order_ref.shape, 1)
    source = blockwise(source, n_tensor, rank // n_tensor, t)
    target = lax.broadcasted_iota(jnp.int32, order_ref.shape, 0)
    order_ref[...] = jnp.where(source == target, 1.0, 0.0).astype(BF)


def block_rows(k, requests):
    return pl.ds(pl.multiple_of((lax.axis_index("adapter") ^ k) * requests, requests), requests)


def shrink_kernel(*refs):
    *blocks, mask_ref, maps_ref, out_ref, total_ref = refs
    requests = blocks[0].shape[0]
    x = jnp.concatenate([b[...] for b in blocks], axis=0)
    mask = jnp.concatenate(
        [mask_ref[block_rows(k, requests), :] for k in range(len(blocks))], axis=0
    )
    total = None
    for j in range(maps_ref.shape[0]):
        part = lax.dot_general(x, maps_ref[j], (((1,), (1,)), ((), ())), preferred_element_type=F32)
        part = jnp.where(mask[:, j : j + 1] > 0, part, 0.0)
        total = part if total is None else total + part
    for k in range(len(blocks)):
        total_ref[block_rows(k, requests), :] = total[k * requests : (k + 1) * requests]
    middle = total.shape[0] // 2
    out_ref[...] = jnp.concatenate([total_ref[:middle], total_ref[middle:]], axis=1).astype(BF)


def load_kernel(*refs):
    *pairs, sems = refs
    count = len(pairs) // 2
    copies = [
        pltpu.make_async_copy(source, target, sems.at[i])
        for i, (source, target) in enumerate(zip(pairs[:count], pairs[count:]))
    ]
    for copy in copies:
        copy.start()
    for copy in copies:
        copy.wait()


def project_kernel(other, *refs):
    *blocks, weight_ref, out_ref = refs
    half = out_ref.shape[1]
    tile = 256 if half % 256 == 0 else 128
    side = lax.rem(lax.axis_index("tensor") + other, 2)
    x = jnp.concatenate([b[...] for b in blocks], axis=0)
    for i in range(half // tile):
        start = pl.multiple_of(side * half + i * tile, tile)
        part = jnp.dot(x, weight_ref[:, pl.ds(start, tile)], preferred_element_type=F32)
        out_ref[:, i * tile : (i + 1) * tile] = part.astype(out_ref.dtype)


def join_kernel(keep_ref, came_ref, out_ref):
    out_ref[...] = (keep_ref[...] + came_ref[...].astype(F32)).astype(BF)


def terms_kernel(n_adapter, n_tensor, *refs):
    parts = refs[:n_tensor]
    select_ref, order_ref = refs[n_tensor : n_tensor + 2]
    maps = refs[n_tensor + 2 : -n_adapter]
    outs = refs[-n_adapter:]
    per_owner = maps[0].shape[1]
    a = lax.axis_index("adapter")
    sums = [p[...].astype(F32) for p in parts]
    while len(sums) > 1:
        sums = [x + y for x, y in zip(sums[::2], sums[1::2])]
    rank = sums[0].shape[1] // 2
    shrunk = jnp.concatenate([sums[0][:, :rank], sums[0][:, rank:]], axis=0).astype(BF)
    held = jnp.dot(select_ref[...], shrunk, preferred_element_type=F32)
    held = jnp.dot(held.astype(BF), order_ref[...], preferred_element_type=F32)
    slot_of = lax.broadcasted_iota(jnp.int32, held.shape, 0) // SLOTS
    wide = jnp.concatenate(
        [jnp.where(slot_of == j, held, 0.0) for j in range(per_owner)], axis=1
    ).astype(BF)
    for k in range(n_adapter):
        up = jnp.concatenate([m[a ^ k, j] for j in range(per_owner) for m in maps], axis=0)
        outs[k][...] = jnp.dot(wide, up, preferred_element_type=F32).astype(BF)


def finish_kernel(requests, place_ref, *refs):
    *base, out_ref = refs
    base, pieces = base[:2], base[2:]
    blocks = range(out_ref.shape[0] // requests)
    received = jnp.concatenate([p[...] for p in pieces], axis=0)
    place = jnp.concatenate([place_ref[block_rows(k, requests), :] for k in blocks], axis=0)
    delta = jnp.dot(place, received, preferred_element_type=F32)
    total = base[0][...].astype(F32) + base[1][...].astype(F32)
    total = (total + ADAPTER_SCALE * delta).astype(BF)
    for k in blocks:
        out_ref[block_rows(k, requests), :] = total[k * requests : (k + 1) * requests]


def make_shards(n_adapter, n_tensor):
    def swap(x, axis, n, k):
        return lax.ppermute(x, axis, [(i, i ^ k) for i in range(n)])

    def shards(
        queries,
        cache_keys,
        cached_value_rows,
        new_keys,
        fresh_value_rows,
        lengths,
        adapter_ids,
        adapter_slots,
        out_weight,
        shrink_weight,
        expand_weight,
    ):
        low = lax.axis_index("tensor") % 2
        per_owner, rank_part, width = expand_weight.shape
        rank = shrink_weight.shape[2]
        columns = out_weight.shape[1]
        half = columns // 2
        requests = queries.shape[0]
        tokens = adapter_ids.shape[0]
        owned = per_owner * SLOTS

        attended = attend(
            queries, cache_keys, cached_value_rows, new_keys, fresh_value_rows, lengths
        )
        blocks = [swap(attended, "adapter", n_adapter, k) for k in range(1, n_adapter)]

        up_shape = jax.ShapeDtypeStruct((n_adapter, per_owner, rank_part, half), BF)
        expand_weight, ids, _ = lax.optimization_barrier(
            (expand_weight, adapter_ids.reshape(1, tokens), attended)
        )
        up_low, up_high = pl.pallas_call(
            split_kernel,
            out_shape=(up_shape, up_shape),
            in_specs=[ANY],
            out_specs=(VMEM, VMEM),
            scratch_shapes=[pltpu.SemaphoreType.DMA((n_adapter, 2))],
            compiler_params=pltpu.CompilerParams(vmem_limit_bytes=16 << 20),
            name="split",
        )(expand_weight)
        maps = [up_low] + [
            swap((up_low, up_high)[k % 2], "tensor", n_tensor, k) for k in range(1, n_tensor)
        ]
        ids, blocks[0] = lax.optimization_barrier((ids, blocks[0]))
        out_weight, maps[1] = lax.optimization_barrier((out_weight, maps[1]))

        loads = (attended, out_weight, jnp.swapaxes(shrink_weight, 1, 2))
        here_block, weight, down = pl.pallas_call(
            load_kernel,
            out_shape=[jax.ShapeDtypeStruct(x.shape, BF) for x in loads],
            in_specs=[ANY] * 3,
            out_specs=[VMEM] * 3,
            scratch_shapes=[pltpu.SemaphoreType.DMA((3,))],
            compiler_params=pltpu.CompilerParams(vmem_limit_bytes=44 << 20),
            cost_estimate=pl.CostEstimate(
                flops=0, bytes_accessed=4 * out_weight.size, transcendentals=0
            ),
            name="load",
        )(*loads)
        blocks = [here_block] + blocks

        here, select, place, reorder = pl.pallas_call(
            functools.partial(ids_kernel, n_adapter, n_tensor),
            out_shape=[
                jax.ShapeDtypeStruct((tokens, per_owner), F32),
                jax.ShapeDtypeStruct((owned, tokens), BF),
                jax.ShapeDtypeStruct((tokens, n_adapter * owned), BF),
                jax.ShapeDtypeStruct((rank, rank), BF),
            ],
            in_specs=[VMEM, SMEM],
            out_specs=[VMEM] * 4,
            compiler_params=pltpu.CompilerParams(vmem_limit_bytes=16 << 20),
            name="ids",
        )(ids, adapter_slots)

        shrunk = pl.pallas_call(
            shrink_kernel,
            out_shape=jax.ShapeDtypeStruct((tokens // 2, 2 * rank), BF),
            in_specs=[VMEM] * (n_adapter + 2),
            out_specs=VMEM,
            scratch_shapes=[pltpu.VMEM((tokens, rank), F32)],
            compiler_params=pltpu.CompilerParams(vmem_limit_bytes=24 << 20),
            name="shrink",
        )(*blocks, here, down)
        shrunk, *blocks = lax.optimization_barrier((shrunk, *blocks))
        shrunk = [shrunk] + [swap(shrunk, "tensor", n_tensor, k) for k in range(1, n_tensor)]

        blocks[0], *maps[2:] = lax.optimization_barrier((blocks[0], *maps[2:]))

        def project(other, dtype):
            return pl.pallas_call(
                functools.partial(project_kernel, other),
                out_shape=jax.ShapeDtypeStruct((tokens, half), dtype),
                in_specs=[VMEM] * (n_adapter + 1),
                out_specs=VMEM,
                compiler_params=pltpu.CompilerParams(vmem_limit_bytes=24 << 20),
                cost_estimate=pl.CostEstimate(
                    flops=tokens * out_weight.size,
                    bytes_accessed=2 * out_weight.size,
                    transcendentals=0,
                ),
                name="project",
            )(*blocks, weight)

        came = swap(project(1, BF), "tensor", n_tensor, 1)
        base = pl.pallas_call(
            join_kernel,
            out_shape=jax.ShapeDtypeStruct((tokens, half), BF),
            in_specs=[VMEM] * 2,
            out_specs=VMEM,
            compiler_params=pltpu.CompilerParams(vmem_limit_bytes=16 << 20),
            name="join",
        )(project(0, F32), came)
        base, *shrunk = lax.optimization_barrier((base, *shrunk))
        step = 2
        while step * 2 < n_tensor:
            other = swap(base, "tensor", n_tensor, step)
            base = (base.astype(F32) + other.astype(F32)).astype(BF)
            step *= 2
        base = [base, swap(base, "tensor", n_tensor, step)]

        terms = pl.pallas_call(
            functools.partial(terms_kernel, n_adapter, n_tensor),
            out_shape=[jax.ShapeDtypeStruct((owned, half), BF)] * n_adapter,
            in_specs=[VMEM] * (2 + n_tensor + len(maps)),
            out_specs=[VMEM] * n_adapter,
            compiler_params=pltpu.CompilerParams(vmem_limit_bytes=24 << 20),
            name="terms",
        )(*shrunk, select, reorder, *maps)
        received = [terms[0]] + [
            swap(terms[k], "adapter", n_adapter, k) for k in range(1, n_adapter)
        ]

        mine = pl.pallas_call(
            functools.partial(finish_kernel, requests),
            out_shape=jax.ShapeDtypeStruct((tokens, half), BF),
            in_specs=[VMEM] * (3 + n_adapter),
            out_specs=VMEM,
            compiler_params=pltpu.CompilerParams(vmem_limit_bytes=24 << 20),
            name="finish",
        )(place, *base, *received)
        other = swap(mine, "tensor", n_tensor, 1)
        return jnp.where(
            low == 0,
            jnp.concatenate([mine, other], axis=1),
            jnp.concatenate([other, mine], axis=1),
        )

    return shards


def plain_attend(queries, cache_keys, cached_value_rows, new_keys, fresh_value_rows, lengths):
    requests = queries.shape[0]
    positions = cache_keys.shape[1]
    kv_local = cache_keys.shape[2] // HEAD_SIZE
    heads_local = queries.shape[1] // HEAD_SIZE
    group_size = heads_local // kv_local
    factor_term = 1.0 / math.sqrt(HEAD_SIZE)
    q = queries.reshape(requests, kv_local, group_size, HEAD_SIZE)
    k = cache_keys.reshape(requests, positions, kv_local, HEAD_SIZE)
    v = cached_value_rows.reshape(requests, positions, kv_local, HEAD_SIZE)
    scores = jnp.einsum("rkgd,rckd->rkgc", q, k, preferred_element_type=F32) * factor_term
    own = (
        jnp.einsum(
            "ivhz,ivz->ivh",
            q,
            new_keys.reshape(requests, kv_local, HEAD_SIZE),
            preferred_element_type=F32,
        )
        * factor_term
    )
    valid = jnp.arange(positions)[None, None, None, :] < lengths[:, None, None, None]
    scores = jnp.where(valid, scores, -jnp.inf)
    row_top = jnp.maximum(jnp.max(scores, axis=-1), own)
    powers = jnp.exp(scores - row_top[..., None])
    own_power = jnp.exp(own - row_top)
    row_total = jnp.sum(powers, axis=-1) + own_power
    weights = (powers / row_total[..., None]).astype(BF)
    own_weight = (own_power / row_total).astype(BF)
    blended = jnp.einsum("rkgc,rckd->rkgd", weights, v, preferred_element_type=F32)
    blended = blended + own_weight.astype(F32)[..., None] * fresh_value_rows.reshape(
        requests, kv_local, 1, HEAD_SIZE
    ).astype(F32)
    return blended.reshape(requests, heads_local * HEAD_SIZE).astype(BF)


def make_plain_shards(n_adapter, n_tensor):
    def swap(x, axis, n, k):
        return lax.ppermute(x, axis, [(i, i ^ k) for i in range(n)])

    def shards(
        queries,
        cache_keys,
        cached_value_rows,
        new_keys,
        fresh_value_rows,
        lengths,
        adapter_ids,
        adapter_slots,
        out_weight,
        shrink_weight,
        expand_weight,
    ):
        a = lax.axis_index("adapter")
        t = lax.axis_index("tensor")
        low = t % 2
        adapters = adapter_slots.shape[0]
        per_owner, rank_part, width = expand_weight.shape
        rank = shrink_weight.shape[2]
        columns = out_weight.shape[1]
        half = columns // 2
        requests = queries.shape[0]
        tokens = adapter_ids.shape[0]
        owned = per_owner * SLOTS

        up = expand_weight.reshape(per_owner, rank_part, n_adapter, 2, half)
        up_keep = lax.dynamic_index_in_dim(up, low, 3, keepdims=False)
        up_send = lax.dynamic_index_in_dim(up, 1 - low, 3, keepdims=False)
        up = jnp.concatenate([up_keep, swap(up_send, "tensor", n_tensor, 1)], axis=1)
        step = 2
        while step < n_tensor:
            up = jnp.concatenate([up, swap(up, "tensor", n_tensor, step)], axis=1)
            step *= 2
        up = up.reshape(per_owner * rank, n_adapter * half)

        attended = plain_attend(
            queries, cache_keys, cached_value_rows, new_keys, fresh_value_rows, lengths
        )

        matches = adapter_ids[:, None] == jnp.arange(adapters, dtype=jnp.int32)[None, :]
        counts = matches.astype(jnp.int32)
        rank_within = jnp.sum(jnp.cumsum(counts, axis=0) * counts, axis=1) - 1
        stored = jnp.sum(counts * adapter_slots[None, :], axis=1)
        owner = stored // per_owner
        slot = (stored % per_owner) * SLOTS + rank_within

        blocks = [attended] + [swap(attended, "adapter", n_adapter, k) for k in range(1, n_adapter)]
        rows = jnp.zeros((tokens, queries.shape[1]), BF)
        for k, block in enumerate(blocks):
            rows = lax.dynamic_update_slice(rows, block, ((a ^ k) * requests, 0))

        parts = jnp.einsum("rd,adn->arn", rows, shrink_weight, preferred_element_type=F32)
        here = stored[None, :] - a * per_owner == jnp.arange(per_owner, dtype=jnp.int32)[:, None]
        shrunk = jnp.sum(jnp.where(here[:, :, None], parts, 0.0), axis=0)
        step = 1
        while step < n_tensor:
            shrunk = shrunk + swap(shrunk, "tensor", n_tensor, step)
            step *= 2
        shrunk = shrunk.astype(BF)

        base = jnp.dot(rows, out_weight, preferred_element_type=F32)
        base_keep = lax.dynamic_slice_in_dim(base, low * half, half, 1)
        base_send = lax.dynamic_slice_in_dim(base, (1 - low) * half, half, 1).astype(BF)
        base = (base_keep + swap(base_send, "tensor", n_tensor, 1).astype(F32)).astype(BF)
        total = base.astype(F32)
        step = 2
        while step < n_tensor:
            total = total + swap(total.astype(BF), "tensor", n_tensor, step).astype(F32)
            step *= 2

        positions = jnp.arange(rank, dtype=jnp.int32)
        source = ((positions // rank_part) ^ t) * rank_part + positions % rank_part
        reorder = (jnp.arange(rank, dtype=jnp.int32)[:, None] == source[None, :]).astype(BF)
        select = (
            (jnp.arange(owned, dtype=jnp.int32)[:, None] == slot[None, :]) & (owner[None, :] == a)
        ).astype(BF)
        held = jnp.dot(jnp.dot(select, shrunk).astype(BF), reorder).astype(BF)
        in_block = (
            jnp.arange(owned, dtype=jnp.int32)[:, None] // SLOTS
            == jnp.arange(per_owner, dtype=jnp.int32)[None, :]
        )
        wide = jnp.where(in_block[:, :, None], held[:, None, :], 0).reshape(owned, -1)
        terms = jnp.dot(wide.astype(BF), up, preferred_element_type=F32).astype(BF)
        received = []
        for k in range(n_adapter):
            piece = lax.dynamic_slice_in_dim(terms, (a ^ k) * half, half, 1)
            received.append(swap(piece, "adapter", n_adapter, k) if k else piece)
        received = jnp.concatenate(received, axis=0)
        place = (
            ((owner ^ a) * owned + slot)[:, None]
            == jnp.arange(n_adapter * owned, dtype=jnp.int32)[None, :]
        ).astype(BF)
        delta = jnp.dot(place, received, preferred_element_type=F32)
        mine = (total + ADAPTER_SCALE * delta).astype(BF)
        other = swap(mine, "tensor", n_tensor, 1)
        return jnp.where(
            low == 0,
            jnp.concatenate([mine, other], axis=1),
            jnp.concatenate([other, mine], axis=1),
        )

    return shards


def solution(mesh):
    in_specs = (
        P(("groups", "adapter"), "tensor"),
        P(("groups", "adapter"), None, "tensor"),
        P(("groups", "adapter"), None, "tensor"),
        P(("groups", "adapter"), "tensor"),
        P(("groups", "adapter"), "tensor"),
        P(("groups", "adapter")),
        P("groups"),
        P(),
        P("tensor", "adapter"),
        P("adapter", "tensor", None),
        P("adapter", "tensor", None),
    )
    out_specs = P("groups", "adapter")
    sizes = mesh.shape["adapter"], mesh.shape["tensor"]
    fast, plain = make_shards(*sizes), make_plain_shards(*sizes)

    def shards(*arrays):
        return (plain if arrays[8].shape[1] % 256 else fast)(*arrays)

    return jax.shard_map(shards, mesh=mesh, in_specs=in_specs, out_specs=out_specs, check_vma=False)
```

```python
import functools
import math

import jax
import jax.numpy as jnp
from jax import lax
from jax.experimental import pallas as pl
from jax.experimental.pallas import tpu as pltpu
from jax.sharding import PartitionSpec as P

HEAD_SIZE = 128
SLOTS = 32
ADAPTER_SCALE = 2.0
BF = jnp.bfloat16
F32 = jnp.float32
VMEM = pl.BlockSpec(memory_space=pltpu.VMEM)
SMEM = pl.BlockSpec(memory_space=pltpu.SMEM)
ANY = pl.BlockSpec(memory_space=pl.ANY)


def attend_kernel(
    chunk,
    length_ref,
    q_hbm,
    k_hbm,
    v_hbm,
    nk_hbm,
    nv_hbm,
    up_hbm,
    out_ref,
    low_hbm,
    high_hbm,
    q_ref,
    k_ref,
    v_ref,
    nk_ref,
    nv_ref,
    low_ref,
    high_ref,
    sems,
    cut_sems,
    put_sems,
):
    half = low_ref.shape[3]
    low = lax.rem(lax.axis_index("tensor"), 2)
    cuts = []
    for b in range(low_ref.shape[0]):
        for i, (ref, side) in enumerate(((low_ref, low), (high_ref, 1 - low))):
            start = pl.multiple_of((2 * b + side) * half, half)
            cuts.append(
                pltpu.make_async_copy(
                    up_hbm.at[:, :, pl.ds(start, half)], ref.at[b], cut_sems.at[b, i]
                )
            )
    requests, positions, kv_width = k_ref.shape
    heads = q_ref.shape[1] // HEAD_SIZE
    kv_heads = kv_width // HEAD_SIZE
    group = heads // kv_heads
    factor = 1.0 / math.sqrt(HEAD_SIZE)
    extended = positions + chunk

    small = [
        pltpu.make_async_copy(source, target, sems.at[2, i])
        for i, (source, target) in enumerate(((q_hbm, q_ref), (nk_hbm, nk_ref), (nv_hbm, nv_ref)))
    ]
    parts = [pl.ds(first, chunk) for first in range(0, requests, chunk)]
    keys = [
        pltpu.make_async_copy(k_hbm.at[part], k_ref.at[part], sems.at[0, i])
        for i, part in enumerate(parts)
    ]
    values = [
        pltpu.make_async_copy(v_hbm.at[part], v_ref.at[part], sems.at[1, i])
        for i, part in enumerate(parts)
    ]
    for copy in small:
        copy.start()
    for key, value in zip(keys, values):
        key.start()
        value.start()
    for copy in cuts:
        copy.start()

    row_group = lax.broadcasted_iota(jnp.int32, (heads, kv_width), 0) // group
    lane_group = lax.broadcasted_iota(jnp.int32, (heads, kv_width), 1) // HEAD_SIZE
    diagonal = row_group == lane_group
    place = lax.broadcasted_iota(jnp.int32, (heads, extended), 1)
    ones = jnp.ones((extended, HEAD_SIZE), BF)
    for copy in small:
        copy.wait()
    puts = [
        pltpu.make_async_copy(low_ref, low_hbm, put_sems.at[0]),
        pltpu.make_async_copy(high_ref, high_hbm, put_sems.at[1]),
    ]
    for c, first in enumerate(range(0, requests, chunk)):
        if first + chunk >= requests:
            for copy in cuts:
                copy.wait()
            for copy in puts:
                copy.start()
        q = q_ref[first : first + chunk].reshape(chunk, heads, HEAD_SIZE)
        new_keys = nk_ref[first : first + chunk]
        new_values = nv_ref[first : first + chunk]
        keys[c].wait()
        scores = []
        for i in range(chunk):
            r = first + i
            wide = jnp.where(
                diagonal, jnp.concatenate([q[i]] * kv_heads, axis=1), jnp.zeros((), BF)
            )
            score = lax.dot_general(
                wide,
                jnp.concatenate([k_ref[r], new_keys], axis=0),
                (((1,), (1,)), ((), ())),
                preferred_element_type=F32,
            )
            valid = (place < length_ref[r]) | (place == positions + i)
            scores.append(jnp.where(valid, score * factor, -jnp.inf))
        scores = jnp.stack(scores).reshape(chunk * heads, extended)
        powers = jnp.exp(scores - jnp.max(scores, axis=1, keepdims=True)).astype(BF)
        inverse = 1.0 / jnp.dot(powers, ones, preferred_element_type=F32)
        values[c].wait()
        outs = []
        for i in range(chunk):
            rows = slice(i * heads, (i + 1) * heads)
            blend = jnp.dot(
                powers[rows],
                jnp.concatenate([v_ref[first + i], new_values], axis=0),
                preferred_element_type=F32,
            )
            blend = jnp.concatenate(
                [
                    blend[g * group : (g + 1) * group, g * HEAD_SIZE : (g + 1) * HEAD_SIZE]
                    for g in range(kv_heads)
                ],
                axis=0,
            )
            outs.append((blend * inverse[rows]).astype(BF))
        out_ref[first : first + chunk] = jnp.stack(outs).reshape(chunk, heads * HEAD_SIZE)
    for copy in puts:
        copy.wait()


def attend(
    queries, cache_keys, cached_value_rows, new_keys, fresh_value_rows, lengths, up, blocks
):
    requests = queries.shape[0]
    chunk = 16 if requests % 16 == 0 else requests
    per_owner, rank_part, width = up.shape
    part = (blocks, per_owner, rank_part, width // (2 * blocks))
    moved = (queries, cache_keys, cached_value_rows, new_keys, fresh_value_rows)
    return pl.pallas_call(
        functools.partial(attend_kernel, chunk),
        out_shape=[jax.ShapeDtypeStruct(shape, BF) for shape in (queries.shape, part, part)],
        in_specs=[SMEM] + [ANY] * 6,
        out_specs=[VMEM, ANY, ANY],
        scratch_shapes=[pltpu.VMEM(shape, BF) for shape in [x.shape for x in moved] + [part, part]]
        + [
            pltpu.SemaphoreType.DMA((3, max(3, requests // chunk))),
            pltpu.SemaphoreType.DMA((blocks, 2)),
            pltpu.SemaphoreType.DMA((2,)),
        ],
        compiler_params=pltpu.CompilerParams(vmem_limit_bytes=60 << 20),
        cost_estimate=pl.CostEstimate(
            flops=8 * queries.size * cache_keys.shape[1],
            bytes_accessed=4 * cache_keys.size,
            transcendentals=queries.size,
        ),
        name="attend",
    )(lengths, *moved, up)


def blockwise(position, count, size, index):
    moved = jnp.zeros_like(position)
    for k in range(count):
        inside = (position >= k * size) & (position < (k + 1) * size)
        moved = jnp.where(inside, position + ((index ^ k) - k) * size, moved)
    return moved


def ids_kernel(n_adapter, n_tensor, ids_ref, slots_ref, here_ref, select_ref, place_ref, order_ref):
    tokens, per_owner = here_ref.shape
    owned = select_ref.shape[0]
    rank = order_ref.shape[0]
    a = lax.axis_index("adapter")
    t = lax.axis_index("tensor")
    down = lax.broadcasted_iota(jnp.int32, (tokens, tokens), 0)
    across = lax.broadcasted_iota(jnp.int32, (tokens, tokens), 1)
    ids_row = ids_ref[...].astype(F32)
    ids_column = jnp.sum(jnp.where(down == across, ids_row, 0.0), axis=1, keepdims=True)
    same = ids_row == ids_column

    def stored(ids):
        return sum(
            jnp.where(ids == j, slots_ref[j].astype(F32), 0.0) for j in range(slots_ref.shape[0])
        )

    earlier = jnp.where(same & (across < down), 1.0, 0.0)
    stored_column = stored(ids_column)
    key_column = stored_column * SLOTS + jnp.sum(earlier, axis=1, keepdims=True)
    earlier = jnp.where(same & (down < across), 1.0, 0.0)
    key_row = stored(ids_row) * SLOTS + jnp.sum(earlier, axis=0, keepdims=True)
    key_column, key_row = key_column.astype(jnp.int32), key_row.astype(jnp.int32)
    adapter = lax.broadcasted_iota(jnp.int32, here_ref.shape, 1) + a * per_owner
    here_ref[...] = jnp.where(adapter == stored_column.astype(jnp.int32), 1.0, 0.0)
    slot = lax.broadcasted_iota(jnp.int32, select_ref.shape, 0) + a * owned
    select_ref[...] = jnp.where(slot == key_row, 1.0, 0.0).astype(BF)
    slot = lax.broadcasted_iota(jnp.int32, place_ref.shape, 1)
    slot = blockwise(slot, n_adapter, owned, a)
    place_ref[...] = jnp.where(slot == key_column, 1.0, 0.0).astype(BF)
    source = lax.broadcasted_iota(jnp.int32, order_ref.shape, 1)
    source = blockwise(source, n_tensor, rank // n_tensor, t)
    target = lax.broadcasted_iota(jnp.int32, order_ref.shape, 0)
    order_ref[...] = jnp.where(source == target, 1.0, 0.0).astype(BF)


def block_rows(k, requests):
    return pl.ds(pl.multiple_of((lax.axis_index("adapter") ^ k) * requests, requests), requests)


def shrink_kernel(*refs):
    *blocks, mask_ref, maps_ref, out_ref, total_ref = refs
    requests = blocks[0].shape[0]
    x = jnp.concatenate([b[...] for b in blocks], axis=0)
    mask = jnp.concatenate(
        [mask_ref[block_rows(k, requests), :] for k in range(len(blocks))], axis=0
    )
    total = None
    for j in range(maps_ref.shape[0]):
        part = lax.dot_general(x, maps_ref[j], (((1,), (1,)), ((), ())), preferred_element_type=F32)
        part = jnp.where(mask[:, j : j + 1] > 0, part, 0.0)
        total = part if total is None else total + part
    for k in range(len(blocks)):
        total_ref[block_rows(k, requests), :] = total[k * requests : (k + 1) * requests]
    middle = total.shape[0] // 2
    out_ref[...] = jnp.concatenate([total_ref[:middle], total_ref[middle:]], axis=1).astype(BF)


def load_kernel(*refs):
    *pairs, sems = refs
    count = len(pairs) // 2
    copies = [
        pltpu.make_async_copy(source, target, sems.at[i])
        for i, (source, target) in enumerate(zip(pairs[:count], pairs[count:]))
    ]
    for copy in copies:
        copy.start()
    for copy in copies:
        copy.wait()


def project_kernel(other, *refs):
    *blocks, weight_ref, out_ref = refs
    half = out_ref.shape[1]
    tile = 256 if half % 256 == 0 else 128
    side = lax.rem(lax.axis_index("tensor") + other, 2)
    x = jnp.concatenate([b[...] for b in blocks], axis=0)
    for i in range(half // tile):
        start = pl.multiple_of(side * half + i * tile, tile)
        part = jnp.dot(x, weight_ref[:, pl.ds(start, tile)], preferred_element_type=F32)
        out_ref[:, i * tile : (i + 1) * tile] = part.astype(out_ref.dtype)


def join_kernel(keep_ref, came_ref, out_ref):
    out_ref[...] = (keep_ref[...] + came_ref[...].astype(F32)).astype(BF)


def terms_kernel(n_adapter, n_tensor, *refs):
    parts = refs[:n_tensor]
    select_ref, order_ref = refs[n_tensor : n_tensor + 2]
    maps = refs[n_tensor + 2 : -n_adapter]
    outs = refs[-n_adapter:]
    per_owner = maps[0].shape[1]
    a = lax.axis_index("adapter")
    sums = [p[...].astype(F32) for p in parts]
    while len(sums) > 1:
        sums = [x + y for x, y in zip(sums[::2], sums[1::2])]
    rank = sums[0].shape[1] // 2
    shrunk = jnp.concatenate([sums[0][:, :rank], sums[0][:, rank:]], axis=0).astype(BF)
    held = jnp.dot(select_ref[...], shrunk, preferred_element_type=F32)
    held = jnp.dot(held.astype(BF), order_ref[...], preferred_element_type=F32)
    slot_of = lax.broadcasted_iota(jnp.int32, held.shape, 0) // SLOTS
    wide = jnp.concatenate(
        [jnp.where(slot_of == j, held, 0.0) for j in range(per_owner)], axis=1
    ).astype(BF)
    for k in range(n_adapter):
        up = jnp.concatenate([m[a ^ k, j] for j in range(per_owner) for m in maps], axis=0)
        outs[k][...] = jnp.dot(wide, up, preferred_element_type=F32).astype(BF)


def finish_kernel(requests, place_ref, *refs):
    *base, out_ref = refs
    base, pieces = base[:2], base[2:]
    blocks = range(out_ref.shape[0] // requests)
    received = jnp.concatenate([p[...] for p in pieces], axis=0)
    place = jnp.concatenate([place_ref[block_rows(k, requests), :] for k in blocks], axis=0)
    delta = jnp.dot(place, received, preferred_element_type=F32)
    total = base[0][...].astype(F32) + base[1][...].astype(F32)
    total = (total + ADAPTER_SCALE * delta).astype(BF)
    for k in blocks:
        out_ref[block_rows(k, requests), :] = total[k * requests : (k + 1) * requests]


def make_shards(n_adapter, n_tensor):
    def swap(x, axis, n, k):
        return lax.ppermute(x, axis, [(i, i ^ k) for i in range(n)])

    def shards(
        queries,
        cache_keys,
        cached_value_rows,
        new_keys,
        fresh_value_rows,
        lengths,
        adapter_ids,
        adapter_slots,
        out_weight,
        shrink_weight,
        expand_weight,
    ):
        low = lax.axis_index("tensor") % 2
        per_owner = expand_weight.shape[0]
        rank = shrink_weight.shape[2]
        columns = out_weight.shape[1]
        half = columns // 2
        requests = queries.shape[0]
        tokens = adapter_ids.shape[0]
        owned = per_owner * SLOTS

        attended, up_low, up_high = attend(
            queries,
            cache_keys,
            cached_value_rows,
            new_keys,
            fresh_value_rows,
            lengths,
            expand_weight,
            n_adapter,
        )
        blocks = [swap(attended, "adapter", n_adapter, k) for k in range(1, n_adapter)]

        maps = [up_low] + [
            swap((up_low, up_high)[k % 2], "tensor", n_tensor, k) for k in range(1, n_tensor)
        ]
        ids = adapter_ids.reshape(1, tokens)
        ids, maps[1] = lax.optimization_barrier((ids, maps[1]))

        here, select, place, reorder = pl.pallas_call(
            functools.partial(ids_kernel, n_adapter, n_tensor),
            out_shape=[
                jax.ShapeDtypeStruct((tokens, per_owner), F32),
                jax.ShapeDtypeStruct((owned, tokens), BF),
                jax.ShapeDtypeStruct((tokens, n_adapter * owned), BF),
                jax.ShapeDtypeStruct((rank, rank), BF),
            ],
            in_specs=[VMEM, SMEM],
            out_specs=[VMEM] * 4,
            compiler_params=pltpu.CompilerParams(vmem_limit_bytes=16 << 20),
            name="ids",
        )(ids, adapter_slots)

        out_weight, here, blocks[0] = lax.optimization_barrier((out_weight, here, blocks[0]))

        loads = (attended, out_weight, jnp.swapaxes(shrink_weight, 1, 2))
        here_block, weight, down = pl.pallas_call(
            load_kernel,
            out_shape=[jax.ShapeDtypeStruct(x.shape, BF) for x in loads],
            in_specs=[ANY] * 3,
            out_specs=[VMEM] * 3,
            scratch_shapes=[pltpu.SemaphoreType.DMA((3,))],
            compiler_params=pltpu.CompilerParams(vmem_limit_bytes=44 << 20),
            cost_estimate=pl.CostEstimate(
                flops=0, bytes_accessed=4 * out_weight.size, transcendentals=0
            ),
            name="load",
        )(*loads)
        blocks = [here_block] + blocks

        shrunk = pl.pallas_call(
            shrink_kernel,
            out_shape=jax.ShapeDtypeStruct((tokens // 2, 2 * rank), BF),
            in_specs=[VMEM] * (n_adapter + 2),
            out_specs=VMEM,
            scratch_shapes=[pltpu.VMEM((tokens, rank), F32)],
            compiler_params=pltpu.CompilerParams(vmem_limit_bytes=24 << 20),
            name="shrink",
        )(*blocks, here, down)
        shrunk, *blocks = lax.optimization_barrier((shrunk, *blocks))
        shrunk = [shrunk] + [swap(shrunk, "tensor", n_tensor, k) for k in range(1, n_tensor)]


        def project(other, dtype):
            return pl.pallas_call(
                functools.partial(project_kernel, other),
                out_shape=jax.ShapeDtypeStruct((tokens, half), dtype),
                in_specs=[VMEM] * (n_adapter + 1),
                out_specs=VMEM,
                compiler_params=pltpu.CompilerParams(vmem_limit_bytes=24 << 20),
                cost_estimate=pl.CostEstimate(
                    flops=tokens * out_weight.size,
                    bytes_accessed=2 * out_weight.size,
                    transcendentals=0,
                ),
                name="project",
            )(*blocks, weight)

        came = swap(project(1, BF), "tensor", n_tensor, 1)
        blocks[0], *maps[2:] = lax.optimization_barrier((blocks[0], *maps[2:]))
        base = pl.pallas_call(
            join_kernel,
            out_shape=jax.ShapeDtypeStruct((tokens, half), BF),
            in_specs=[VMEM] * 2,
            out_specs=VMEM,
            compiler_params=pltpu.CompilerParams(vmem_limit_bytes=16 << 20),
            name="join",
        )(project(0, F32), came)
        base, *shrunk = lax.optimization_barrier((base, *shrunk))
        step = 2
        while step * 2 < n_tensor:
            other = swap(base, "tensor", n_tensor, step)
            base = (base.astype(F32) + other.astype(F32)).astype(BF)
            step *= 2
        base = [base, swap(base, "tensor", n_tensor, step)]

        terms = pl.pallas_call(
            functools.partial(terms_kernel, n_adapter, n_tensor),
            out_shape=[jax.ShapeDtypeStruct((owned, half), BF)] * n_adapter,
            in_specs=[VMEM] * (2 + n_tensor + len(maps)),
            out_specs=[VMEM] * n_adapter,
            compiler_params=pltpu.CompilerParams(vmem_limit_bytes=24 << 20),
            name="terms",
        )(*shrunk, select, reorder, *maps)
        received = [terms[0]] + [
            swap(terms[k], "adapter", n_adapter, k) for k in range(1, n_adapter)
        ]

        mine = pl.pallas_call(
            functools.partial(finish_kernel, requests),
            out_shape=jax.ShapeDtypeStruct((tokens, half), BF),
            in_specs=[VMEM] * (3 + n_adapter),
            out_specs=VMEM,
            compiler_params=pltpu.CompilerParams(vmem_limit_bytes=24 << 20),
            name="finish",
        )(place, *base, *received)
        other = swap(mine, "tensor", n_tensor, 1)
        return jnp.where(
            low == 0,
            jnp.concatenate([mine, other], axis=1),
            jnp.concatenate([other, mine], axis=1),
        )

    return shards


def plain_attend(queries, cache_keys, cached_value_rows, new_keys, fresh_value_rows, lengths):
    requests = queries.shape[0]
    positions = cache_keys.shape[1]
    kv_local = cache_keys.shape[2] // HEAD_SIZE
    heads_local = queries.shape[1] // HEAD_SIZE
    group_size = heads_local // kv_local
    factor_term = 1.0 / math.sqrt(HEAD_SIZE)
    q = queries.reshape(requests, kv_local, group_size, HEAD_SIZE)
    k = cache_keys.reshape(requests, positions, kv_local, HEAD_SIZE)
    v = cached_value_rows.reshape(requests, positions, kv_local, HEAD_SIZE)
    scores = jnp.einsum("rkgd,rckd->rkgc", q, k, preferred_element_type=F32) * factor_term
    own = (
        jnp.einsum(
            "ivhz,ivz->ivh",
            q,
            new_keys.reshape(requests, kv_local, HEAD_SIZE),
            preferred_element_type=F32,
        )
        * factor_term
    )
    valid = jnp.arange(positions)[None, None, None, :] < lengths[:, None, None, None]
    scores = jnp.where(valid, scores, -jnp.inf)
    row_top = jnp.maximum(jnp.max(scores, axis=-1), own)
    powers = jnp.exp(scores - row_top[..., None])
    own_power = jnp.exp(own - row_top)
    row_total = jnp.sum(powers, axis=-1) + own_power
    weights = (powers / row_total[..., None]).astype(BF)
    own_weight = (own_power / row_total).astype(BF)
    blended = jnp.einsum("rkgc,rckd->rkgd", weights, v, preferred_element_type=F32)
    blended = blended + own_weight.astype(F32)[..., None] * fresh_value_rows.reshape(
        requests, kv_local, 1, HEAD_SIZE
    ).astype(F32)
    return blended.reshape(requests, heads_local * HEAD_SIZE).astype(BF)


def make_plain_shards(n_adapter, n_tensor):
    def swap(x, axis, n, k):
        return lax.ppermute(x, axis, [(i, i ^ k) for i in range(n)])

    def shards(
        queries,
        cache_keys,
        cached_value_rows,
        new_keys,
        fresh_value_rows,
        lengths,
        adapter_ids,
        adapter_slots,
        out_weight,
        shrink_weight,
        expand_weight,
    ):
        a = lax.axis_index("adapter")
        t = lax.axis_index("tensor")
        low = t % 2
        adapters = adapter_slots.shape[0]
        per_owner, rank_part, width = expand_weight.shape
        rank = shrink_weight.shape[2]
        columns = out_weight.shape[1]
        half = columns // 2
        requests = queries.shape[0]
        tokens = adapter_ids.shape[0]
        owned = per_owner * SLOTS

        up = expand_weight.reshape(per_owner, rank_part, n_adapter, 2, half)
        up_keep = lax.dynamic_index_in_dim(up, low, 3, keepdims=False)
        up_send = lax.dynamic_index_in_dim(up, 1 - low, 3, keepdims=False)
        up = jnp.concatenate([up_keep, swap(up_send, "tensor", n_tensor, 1)], axis=1)
        step = 2
        while step < n_tensor:
            up = jnp.concatenate([up, swap(up, "tensor", n_tensor, step)], axis=1)
            step *= 2
        up = up.reshape(per_owner * rank, n_adapter * half)

        attended = plain_attend(
            queries, cache_keys, cached_value_rows, new_keys, fresh_value_rows, lengths
        )

        matches = adapter_ids[:, None] == jnp.arange(adapters, dtype=jnp.int32)[None, :]
        counts = matches.astype(jnp.int32)
        rank_within = jnp.sum(jnp.cumsum(counts, axis=0) * counts, axis=1) - 1
        stored = jnp.sum(counts * adapter_slots[None, :], axis=1)
        owner = stored // per_owner
        slot = (stored % per_owner) * SLOTS + rank_within

        blocks = [attended] + [swap(attended, "adapter", n_adapter, k) for k in range(1, n_adapter)]
        rows = jnp.zeros((tokens, queries.shape[1]), BF)
        for k, block in enumerate(blocks):
            rows = lax.dynamic_update_slice(rows, block, ((a ^ k) * requests, 0))

        parts = jnp.einsum("rd,adn->arn", rows, shrink_weight, preferred_element_type=F32)
        here = stored[None, :] - a * per_owner == jnp.arange(per_owner, dtype=jnp.int32)[:, None]
        shrunk = jnp.sum(jnp.where(here[:, :, None], parts, 0.0), axis=0)
        step = 1
        while step < n_tensor:
            shrunk = shrunk + swap(shrunk, "tensor", n_tensor, step)
            step *= 2
        shrunk = shrunk.astype(BF)

        base = jnp.dot(rows, out_weight, preferred_element_type=F32)
        base_keep = lax.dynamic_slice_in_dim(base, low * half, half, 1)
        base_send = lax.dynamic_slice_in_dim(base, (1 - low) * half, half, 1).astype(BF)
        base = (base_keep + swap(base_send, "tensor", n_tensor, 1).astype(F32)).astype(BF)
        total = base.astype(F32)
        step = 2
        while step < n_tensor:
            total = total + swap(total.astype(BF), "tensor", n_tensor, step).astype(F32)
            step *= 2

        positions = jnp.arange(rank, dtype=jnp.int32)
        source = ((positions // rank_part) ^ t) * rank_part + positions % rank_part
        reorder = (jnp.arange(rank, dtype=jnp.int32)[:, None] == source[None, :]).astype(BF)
        select = (
            (jnp.arange(owned, dtype=jnp.int32)[:, None] == slot[None, :]) & (owner[None, :] == a)
        ).astype(BF)
        held = jnp.dot(jnp.dot(select, shrunk).astype(BF), reorder).astype(BF)
        in_block = (
            jnp.arange(owned, dtype=jnp.int32)[:, None] // SLOTS
            == jnp.arange(per_owner, dtype=jnp.int32)[None, :]
        )
        wide = jnp.where(in_block[:, :, None], held[:, None, :], 0).reshape(owned, -1)
        terms = jnp.dot(wide.astype(BF), up, preferred_element_type=F32).astype(BF)
        received = []
        for k in range(n_adapter):
            piece = lax.dynamic_slice_in_dim(terms, (a ^ k) * half, half, 1)
            received.append(swap(piece, "adapter", n_adapter, k) if k else piece)
        received = jnp.concatenate(received, axis=0)
        place = (
            ((owner ^ a) * owned + slot)[:, None]
            == jnp.arange(n_adapter * owned, dtype=jnp.int32)[None, :]
        ).astype(BF)
        delta = jnp.dot(place, received, preferred_element_type=F32)
        mine = (total + ADAPTER_SCALE * delta).astype(BF)
        other = swap(mine, "tensor", n_tensor, 1)
        return jnp.where(
            low == 0,
            jnp.concatenate([mine, other], axis=1),
            jnp.concatenate([other, mine], axis=1),
        )

    return shards


def solution(mesh):
    in_specs = (
        P(("groups", "adapter"), "tensor"),
        P(("groups", "adapter"), None, "tensor"),
        P(("groups", "adapter"), None, "tensor"),
        P(("groups", "adapter"), "tensor"),
        P(("groups", "adapter"), "tensor"),
        P(("groups", "adapter")),
        P("groups"),
        P(),
        P("tensor", "adapter"),
        P("adapter", "tensor", None),
        P("adapter", "tensor", None),
    )
    out_specs = P("groups", "adapter")
    sizes = mesh.shape["adapter"], mesh.shape["tensor"]
    fast, plain = make_shards(*sizes), make_plain_shards(*sizes)

    def shards(*arrays):
        return (plain if arrays[8].shape[1] % 256 else fast)(*arrays)

    return jax.shard_map(shards, mesh=mesh, in_specs=in_specs, out_specs=out_specs, check_vma=False)
```

```python
import functools
import math

import jax
import jax.numpy as jnp
from jax import lax
from jax.experimental import pallas as pl
from jax.experimental.pallas import tpu as pltpu
from jax.sharding import PartitionSpec as P

HEAD_SIZE = 128
SLOTS = 32
ADAPTER_SCALE = 2.0
BF = jnp.bfloat16
F32 = jnp.float32
VMEM = pl.BlockSpec(memory_space=pltpu.VMEM)
SMEM = pl.BlockSpec(memory_space=pltpu.SMEM)
ANY = pl.BlockSpec(memory_space=pl.ANY)


def attend_kernel(
    chunk,
    length_ref,
    q_hbm,
    k_hbm,
    v_hbm,
    nk_hbm,
    nv_hbm,
    up_hbm,
    out_ref,
    low_hbm,
    high_hbm,
    q_ref,
    k_ref,
    v_ref,
    nk_ref,
    nv_ref,
    low_ref,
    high_ref,
    sems,
    cut_sems,
    put_sems,
):
    half = low_ref.shape[3]
    low = lax.rem(lax.axis_index("tensor"), 2)
    cuts = []
    for b in range(low_ref.shape[0]):
        for i, (ref, side) in enumerate(((low_ref, low), (high_ref, 1 - low))):
            start = pl.multiple_of((2 * b + side) * half, half)
            cuts.append(
                pltpu.make_async_copy(
                    up_hbm.at[:, :, pl.ds(start, half)], ref.at[b], cut_sems.at[b, i]
                )
            )
    requests, positions, kv_width = k_ref.shape
    heads = q_ref.shape[1] // HEAD_SIZE
    kv_heads = kv_width // HEAD_SIZE
    group = heads // kv_heads
    factor = 1.0 / math.sqrt(HEAD_SIZE)
    extended = positions + chunk

    small = [
        pltpu.make_async_copy(source, target, sems.at[2, i])
        for i, (source, target) in enumerate(((q_hbm, q_ref), (nk_hbm, nk_ref), (nv_hbm, nv_ref)))
    ]
    parts = [pl.ds(first, chunk) for first in range(0, requests, chunk)]
    keys = [
        pltpu.make_async_copy(k_hbm.at[part], k_ref.at[part], sems.at[0, i])
        for i, part in enumerate(parts)
    ]
    values = [
        pltpu.make_async_copy(v_hbm.at[part], v_ref.at[part], sems.at[1, i])
        for i, part in enumerate(parts)
    ]
    for copy in small:
        copy.start()
    for key, value in zip(keys, values):
        key.start()
        value.start()
    for copy in cuts:
        copy.start()

    row_group = lax.broadcasted_iota(jnp.int32, (heads, kv_width), 0) // group
    lane_group = lax.broadcasted_iota(jnp.int32, (heads, kv_width), 1) // HEAD_SIZE
    diagonal = row_group == lane_group
    place = lax.broadcasted_iota(jnp.int32, (heads, extended), 1)
    ones = jnp.ones((extended, HEAD_SIZE), BF)
    for copy in small:
        copy.wait()
    puts = [
        pltpu.make_async_copy(low_ref, low_hbm, put_sems.at[0]),
        pltpu.make_async_copy(high_ref, high_hbm, put_sems.at[1]),
    ]
    for c, first in enumerate(range(0, requests, chunk)):
        if first + chunk >= requests:
            for copy in cuts:
                copy.wait()
            for copy in puts:
                copy.start()
        q = q_ref[first : first + chunk].reshape(chunk, heads, HEAD_SIZE)
        new_keys = nk_ref[first : first + chunk]
        new_values = nv_ref[first : first + chunk]
        keys[c].wait()
        scores = []
        for i in range(chunk):
            r = first + i
            wide = jnp.where(
                diagonal, jnp.concatenate([q[i]] * kv_heads, axis=1), jnp.zeros((), BF)
            )
            score = lax.dot_general(
                wide,
                jnp.concatenate([k_ref[r], new_keys], axis=0),
                (((1,), (1,)), ((), ())),
                preferred_element_type=F32,
            )
            valid = (place < length_ref[r]) | (place == positions + i)
            scores.append(jnp.where(valid, score * factor, -jnp.inf))
        scores = jnp.stack(scores).reshape(chunk * heads, extended)
        powers = jnp.exp(scores - jnp.max(scores, axis=1, keepdims=True)).astype(BF)
        inverse = 1.0 / jnp.dot(powers, ones, preferred_element_type=F32)
        values[c].wait()
        outs = []
        for i in range(chunk):
            rows = slice(i * heads, (i + 1) * heads)
            blend = jnp.dot(
                powers[rows],
                jnp.concatenate([v_ref[first + i], new_values], axis=0),
                preferred_element_type=F32,
            )
            blend = jnp.concatenate(
                [
                    blend[g * group : (g + 1) * group, g * HEAD_SIZE : (g + 1) * HEAD_SIZE]
                    for g in range(kv_heads)
                ],
                axis=0,
            )
            outs.append((blend * inverse[rows]).astype(BF))
        out_ref[first : first + chunk] = jnp.stack(outs).reshape(chunk, heads * HEAD_SIZE)
    for copy in puts:
        copy.wait()


def attend(
    queries, cache_keys, cached_value_rows, new_keys, fresh_value_rows, lengths, up, blocks
):
    requests = queries.shape[0]
    chunk = 16 if requests % 16 == 0 else requests
    per_owner, rank_part, width = up.shape
    part = (blocks, per_owner, rank_part, width // (2 * blocks))
    moved = (queries, cache_keys, cached_value_rows, new_keys, fresh_value_rows)
    return pl.pallas_call(
        functools.partial(attend_kernel, chunk),
        out_shape=[jax.ShapeDtypeStruct(shape, BF) for shape in (queries.shape, part, part)],
        in_specs=[SMEM] + [ANY] * 6,
        out_specs=[VMEM, ANY, ANY],
        scratch_shapes=[pltpu.VMEM(shape, BF) for shape in [x.shape for x in moved] + [part, part]]
        + [
            pltpu.SemaphoreType.DMA((3, max(3, requests // chunk))),
            pltpu.SemaphoreType.DMA((blocks, 2)),
            pltpu.SemaphoreType.DMA((2,)),
        ],
        compiler_params=pltpu.CompilerParams(vmem_limit_bytes=60 << 20),
        cost_estimate=pl.CostEstimate(
            flops=8 * queries.size * cache_keys.shape[1],
            bytes_accessed=4 * cache_keys.size,
            transcendentals=queries.size,
        ),
        name="attend",
    )(lengths, *moved, up)


def blockwise(position, count, size, index):
    moved = jnp.zeros_like(position)
    for k in range(count):
        inside = (position >= k * size) & (position < (k + 1) * size)
        moved = jnp.where(inside, position + ((index ^ k) - k) * size, moved)
    return moved


def ids_kernel(n_adapter, n_tensor, ids_ref, slots_ref, here_ref, select_ref, place_ref, order_ref):
    tokens, per_owner = here_ref.shape
    owned = select_ref.shape[0]
    rank = order_ref.shape[0]
    a = lax.axis_index("adapter")
    t = lax.axis_index("tensor")
    down = lax.broadcasted_iota(jnp.int32, (tokens, tokens), 0)
    across = lax.broadcasted_iota(jnp.int32, (tokens, tokens), 1)
    ids_row = ids_ref[...].astype(F32)
    ids_column = jnp.sum(jnp.where(down == across, ids_row, 0.0), axis=1, keepdims=True)
    same = ids_row == ids_column

    def stored(ids):
        return sum(
            jnp.where(ids == j, slots_ref[j].astype(F32), 0.0) for j in range(slots_ref.shape[0])
        )

    earlier = jnp.where(same & (across < down), 1.0, 0.0)
    stored_column = stored(ids_column)
    key_column = stored_column * SLOTS + jnp.sum(earlier, axis=1, keepdims=True)
    earlier = jnp.where(same & (down < across), 1.0, 0.0)
    key_row = stored(ids_row) * SLOTS + jnp.sum(earlier, axis=0, keepdims=True)
    key_column, key_row = key_column.astype(jnp.int32), key_row.astype(jnp.int32)
    adapter = lax.broadcasted_iota(jnp.int32, here_ref.shape, 1) + a * per_owner
    here_ref[...] = jnp.where(adapter == stored_column.astype(jnp.int32), 1.0, 0.0)
    slot = lax.broadcasted_iota(jnp.int32, select_ref.shape, 0) + a * owned
    select_ref[...] = jnp.where(slot == key_row, 1.0, 0.0).astype(BF)
    slot = lax.broadcasted_iota(jnp.int32, place_ref.shape, 1)
    slot = blockwise(slot, n_adapter, owned, a)
    place_ref[...] = jnp.where(slot == key_column, 1.0, 0.0).astype(BF)
    source = lax.broadcasted_iota(jnp.int32, order_ref.shape, 1)
    source = blockwise(source, n_tensor, rank // n_tensor, t)
    target = lax.broadcasted_iota(jnp.int32, order_ref.shape, 0)
    order_ref[...] = jnp.where(source == target, 1.0, 0.0).astype(BF)


def block_rows(k, requests):
    return pl.ds(pl.multiple_of((lax.axis_index("adapter") ^ k) * requests, requests), requests)


def shrink_kernel(*refs):
    *blocks, mask_ref, maps_ref, out_ref, total_ref = refs
    requests = blocks[0].shape[0]
    x = jnp.concatenate([b[...] for b in blocks], axis=0)
    mask = jnp.concatenate(
        [mask_ref[block_rows(k, requests), :] for k in range(len(blocks))], axis=0
    )
    total = None
    for j in range(maps_ref.shape[0]):
        part = lax.dot_general(x, maps_ref[j], (((1,), (1,)), ((), ())), preferred_element_type=F32)
        part = jnp.where(mask[:, j : j + 1] > 0, part, 0.0)
        total = part if total is None else total + part
    for k in range(len(blocks)):
        total_ref[block_rows(k, requests), :] = total[k * requests : (k + 1) * requests]
    middle = total.shape[0] // 2
    out_ref[...] = jnp.concatenate([total_ref[:middle], total_ref[middle:]], axis=1)


def load_kernel(*refs):
    *pairs, sems = refs
    count = len(pairs) // 2
    copies = [
        pltpu.make_async_copy(source, target, sems.at[i])
        for i, (source, target) in enumerate(zip(pairs[:count], pairs[count:]))
    ]
    for copy in copies:
        copy.start()
    for copy in copies:
        copy.wait()


def project_kernel(other, *refs):
    *blocks, weight_ref, out_ref = refs
    half = out_ref.shape[1]
    tile = 256 if half % 256 == 0 else 128
    side = lax.rem(lax.axis_index("tensor") + other, 2)
    x = jnp.concatenate([b[...] for b in blocks], axis=0)
    for i in range(half // tile):
        start = pl.multiple_of(side * half + i * tile, tile)
        part = jnp.dot(x, weight_ref[:, pl.ds(start, tile)], preferred_element_type=F32)
        out_ref[:, i * tile : (i + 1) * tile] = part.astype(out_ref.dtype)


def join_kernel(keep_ref, came_ref, *out_refs):
    rows = out_refs[0].shape[0]
    for i, out_ref in enumerate(out_refs):
        part = slice(i * rows, (i + 1) * rows)
        out_ref[...] = (keep_ref[part] + came_ref[part].astype(F32)).astype(BF)


def terms_kernel(n_adapter, n_parts, *refs):
    parts = refs[:n_parts]
    select_ref, order_ref = refs[n_parts : n_parts + 2]
    maps = refs[n_parts + 2 : -n_adapter]
    outs = refs[-n_adapter:]
    per_owner = maps[0].shape[1]
    a = lax.axis_index("adapter")
    sums = [p[...].astype(F32) for p in parts]
    while len(sums) > 1:
        sums = [x + y for x, y in zip(sums[::2], sums[1::2])]
    rank = sums[0].shape[1] // 2
    shrunk = jnp.concatenate([sums[0][:, :rank], sums[0][:, rank:]], axis=0).astype(BF)
    held = jnp.dot(select_ref[...], shrunk, preferred_element_type=F32)
    held = jnp.dot(held.astype(BF), order_ref[...], preferred_element_type=F32)
    slot_of = lax.broadcasted_iota(jnp.int32, held.shape, 0) // SLOTS
    wide = jnp.concatenate(
        [jnp.where(slot_of == j, held, 0.0) for j in range(per_owner)], axis=1
    ).astype(BF)
    for k in range(n_adapter):
        up = jnp.concatenate([m[a ^ k, j] for j in range(per_owner) for m in maps], axis=0)
        outs[k][...] = jnp.dot(wide, up, preferred_element_type=F32).astype(BF)


def finish_kernel(requests, place_ref, *refs):
    *base, out_ref = refs
    base, pieces = base[:4], base[4:]
    blocks = range(out_ref.shape[0] // requests)
    received = jnp.concatenate([p[...] for p in pieces], axis=0)
    place = jnp.concatenate([place_ref[block_rows(k, requests), :] for k in blocks], axis=0)
    delta = jnp.dot(place, received, preferred_element_type=F32)
    base = [b[...].astype(F32) for b in base]
    total = jnp.concatenate([base[0] + base[1], base[2] + base[3]], axis=0)
    total = (total + ADAPTER_SCALE * delta).astype(BF)
    for k in blocks:
        out_ref[block_rows(k, requests), :] = total[k * requests : (k + 1) * requests]


def make_shards(n_adapter, n_tensor):
    def swap(x, axis, n, k):
        return lax.ppermute(x, axis, [(i, i ^ k) for i in range(n)])

    def shards(
        queries,
        cache_keys,
        cached_value_rows,
        new_keys,
        fresh_value_rows,
        lengths,
        adapter_ids,
        adapter_slots,
        out_weight,
        shrink_weight,
        expand_weight,
    ):
        low = lax.axis_index("tensor") % 2
        per_owner = expand_weight.shape[0]
        rank = shrink_weight.shape[2]
        columns = out_weight.shape[1]
        half = columns // 2
        requests = queries.shape[0]
        tokens = adapter_ids.shape[0]
        owned = per_owner * SLOTS

        attended, up_low, up_high = attend(
            queries,
            cache_keys,
            cached_value_rows,
            new_keys,
            fresh_value_rows,
            lengths,
            expand_weight,
            n_adapter,
        )
        blocks = [swap(attended, "adapter", n_adapter, k) for k in range(1, n_adapter)]

        maps = [up_low] + [
            swap((up_low, up_high)[k % 2], "tensor", n_tensor, k) for k in range(1, n_tensor)
        ]
        ids = adapter_ids.reshape(1, tokens)
        ids, maps[1] = lax.optimization_barrier((ids, maps[1]))

        here, select, place, reorder = pl.pallas_call(
            functools.partial(ids_kernel, n_adapter, n_tensor),
            out_shape=[
                jax.ShapeDtypeStruct((tokens, per_owner), F32),
                jax.ShapeDtypeStruct((owned, tokens), BF),
                jax.ShapeDtypeStruct((tokens, n_adapter * owned), BF),
                jax.ShapeDtypeStruct((rank, rank), BF),
            ],
            in_specs=[VMEM, SMEM],
            out_specs=[VMEM] * 4,
            compiler_params=pltpu.CompilerParams(vmem_limit_bytes=16 << 20),
            name="ids",
        )(ids, adapter_slots)

        out_weight, here, blocks[0] = lax.optimization_barrier((out_weight, here, blocks[0]))

        loads = (attended, out_weight, jnp.swapaxes(shrink_weight, 1, 2))
        here_block, weight, down = pl.pallas_call(
            load_kernel,
            out_shape=[jax.ShapeDtypeStruct(x.shape, BF) for x in loads],
            in_specs=[ANY] * 3,
            out_specs=[VMEM] * 3,
            scratch_shapes=[pltpu.SemaphoreType.DMA((3,))],
            compiler_params=pltpu.CompilerParams(vmem_limit_bytes=44 << 20),
            cost_estimate=pl.CostEstimate(
                flops=0, bytes_accessed=4 * out_weight.size, transcendentals=0
            ),
            name="load",
        )(*loads)
        blocks = [here_block] + blocks

        shrunk = pl.pallas_call(
            shrink_kernel,
            out_shape=jax.ShapeDtypeStruct((tokens // 2, 2 * rank), F32),
            in_specs=[VMEM] * (n_adapter + 2),
            out_specs=VMEM,
            scratch_shapes=[pltpu.VMEM((tokens, rank), F32)],
            compiler_params=pltpu.CompilerParams(vmem_limit_bytes=24 << 20),
            name="shrink",
        )(*blocks, here, down)
        shrunk, *blocks = lax.optimization_barrier((shrunk, *blocks))
        shrunk = (shrunk + swap(shrunk, "tensor", n_tensor, 1)).astype(BF)
        shrunk = [shrunk] + [swap(shrunk, "tensor", n_tensor, k) for k in range(2, n_tensor, 2)]


        def project(other, dtype):
            return pl.pallas_call(
                functools.partial(project_kernel, other),
                out_shape=jax.ShapeDtypeStruct((tokens, half), dtype),
                in_specs=[VMEM] * (n_adapter + 1),
                out_specs=VMEM,
                compiler_params=pltpu.CompilerParams(vmem_limit_bytes=24 << 20),
                cost_estimate=pl.CostEstimate(
                    flops=tokens * out_weight.size,
                    bytes_accessed=2 * out_weight.size,
                    transcendentals=0,
                ),
                name="project",
            )(*blocks, weight)

        came = swap(project(1, BF), "tensor", n_tensor, 1)
        base = pl.pallas_call(
            join_kernel,
            out_shape=[jax.ShapeDtypeStruct((tokens // 2, half), BF)] * 2,
            in_specs=[VMEM] * 2,
            out_specs=[VMEM] * 2,
            compiler_params=pltpu.CompilerParams(vmem_limit_bytes=16 << 20),
            name="join",
        )(project(0, F32), came)
        base = list(lax.optimization_barrier((*base, *shrunk)))
        base, shrunk = base[:2], base[2:]

        terms = pl.pallas_call(
            functools.partial(terms_kernel, n_adapter, len(shrunk)),
            out_shape=[jax.ShapeDtypeStruct((owned, half), BF)] * n_adapter,
            in_specs=[VMEM] * (2 + len(shrunk) + len(maps)),
            out_specs=[VMEM] * n_adapter,
            compiler_params=pltpu.CompilerParams(vmem_limit_bytes=24 << 20),
            name="terms",
        )(*shrunk, select, reorder, *maps)
        received = [terms[0]] + [
            swap(terms[k], "adapter", n_adapter, k) for k in range(1, n_adapter)
        ]

        sums = []
        for part in base:
            step = 2
            while step * 2 < n_tensor:
                other = swap(part, "tensor", n_tensor, step)
                part = (part.astype(F32) + other.astype(F32)).astype(BF)
                step *= 2
            sums += [part, swap(part, "tensor", n_tensor, step)]

        mine = pl.pallas_call(
            functools.partial(finish_kernel, requests),
            out_shape=jax.ShapeDtypeStruct((tokens, half), BF),
            in_specs=[VMEM] * (5 + n_adapter),
            out_specs=VMEM,
            compiler_params=pltpu.CompilerParams(vmem_limit_bytes=24 << 20),
            name="finish",
        )(place, *sums, *received)
        other = swap(mine, "tensor", n_tensor, 1)
        return jnp.where(
            low == 0,
            jnp.concatenate([mine, other], axis=1),
            jnp.concatenate([other, mine], axis=1),
        )

    return shards


def plain_attend(queries, cache_keys, cached_value_rows, new_keys, fresh_value_rows, lengths):
    requests = queries.shape[0]
    positions = cache_keys.shape[1]
    kv_local = cache_keys.shape[2] // HEAD_SIZE
    heads_local = queries.shape[1] // HEAD_SIZE
    group_size = heads_local // kv_local
    factor_term = 1.0 / math.sqrt(HEAD_SIZE)
    q = queries.reshape(requests, kv_local, group_size, HEAD_SIZE)
    k = cache_keys.reshape(requests, positions, kv_local, HEAD_SIZE)
    v = cached_value_rows.reshape(requests, positions, kv_local, HEAD_SIZE)
    scores = jnp.einsum("rkgd,rckd->rkgc", q, k, preferred_element_type=F32) * factor_term
    own = (
        jnp.einsum(
            "ivhz,ivz->ivh",
            q,
            new_keys.reshape(requests, kv_local, HEAD_SIZE),
            preferred_element_type=F32,
        )
        * factor_term
    )
    valid = jnp.arange(positions)[None, None, None, :] < lengths[:, None, None, None]
    scores = jnp.where(valid, scores, -jnp.inf)
    row_top = jnp.maximum(jnp.max(scores, axis=-1), own)
    powers = jnp.exp(scores - row_top[..., None])
    own_power = jnp.exp(own - row_top)
    row_total = jnp.sum(powers, axis=-1) + own_power
    weights = (powers / row_total[..., None]).astype(BF)
    own_weight = (own_power / row_total).astype(BF)
    blended = jnp.einsum("rkgc,rckd->rkgd", weights, v, preferred_element_type=F32)
    blended = blended + own_weight.astype(F32)[..., None] * fresh_value_rows.reshape(
        requests, kv_local, 1, HEAD_SIZE
    ).astype(F32)
    return blended.reshape(requests, heads_local * HEAD_SIZE).astype(BF)


def make_plain_shards(n_adapter, n_tensor):
    def swap(x, axis, n, k):
        return lax.ppermute(x, axis, [(i, i ^ k) for i in range(n)])

    def shards(
        queries,
        cache_keys,
        cached_value_rows,
        new_keys,
        fresh_value_rows,
        lengths,
        adapter_ids,
        adapter_slots,
        out_weight,
        shrink_weight,
        expand_weight,
    ):
        a = lax.axis_index("adapter")
        t = lax.axis_index("tensor")
        low = t % 2
        adapters = adapter_slots.shape[0]
        per_owner, rank_part, width = expand_weight.shape
        rank = shrink_weight.shape[2]
        columns = out_weight.shape[1]
        half = columns // 2
        requests = queries.shape[0]
        tokens = adapter_ids.shape[0]
        owned = per_owner * SLOTS

        up = expand_weight.reshape(per_owner, rank_part, n_adapter, 2, half)
        up_keep = lax.dynamic_index_in_dim(up, low, 3, keepdims=False)
        up_send = lax.dynamic_index_in_dim(up, 1 - low, 3, keepdims=False)
        up = jnp.concatenate([up_keep, swap(up_send, "tensor", n_tensor, 1)], axis=1)
        step = 2
        while step < n_tensor:
            up = jnp.concatenate([up, swap(up, "tensor", n_tensor, step)], axis=1)
            step *= 2
        up = up.reshape(per_owner * rank, n_adapter * half)

        attended = plain_attend(
            queries, cache_keys, cached_value_rows, new_keys, fresh_value_rows, lengths
        )

        matches = adapter_ids[:, None] == jnp.arange(adapters, dtype=jnp.int32)[None, :]
        counts = matches.astype(jnp.int32)
        rank_within = jnp.sum(jnp.cumsum(counts, axis=0) * counts, axis=1) - 1
        stored = jnp.sum(counts * adapter_slots[None, :], axis=1)
        owner = stored // per_owner
        slot = (stored % per_owner) * SLOTS + rank_within

        blocks = [attended] + [swap(attended, "adapter", n_adapter, k) for k in range(1, n_adapter)]
        rows = jnp.zeros((tokens, queries.shape[1]), BF)
        for k, block in enumerate(blocks):
            rows = lax.dynamic_update_slice(rows, block, ((a ^ k) * requests, 0))

        parts = jnp.einsum("rd,adn->arn", rows, shrink_weight, preferred_element_type=F32)
        here = stored[None, :] - a * per_owner == jnp.arange(per_owner, dtype=jnp.int32)[:, None]
        shrunk = jnp.sum(jnp.where(here[:, :, None], parts, 0.0), axis=0)
        step = 1
        while step < n_tensor:
            shrunk = shrunk + swap(shrunk, "tensor", n_tensor, step)
            step *= 2
        shrunk = shrunk.astype(BF)

        base = jnp.dot(rows, out_weight, preferred_element_type=F32)
        base_keep = lax.dynamic_slice_in_dim(base, low * half, half, 1)
        base_send = lax.dynamic_slice_in_dim(base, (1 - low) * half, half, 1).astype(BF)
        base = (base_keep + swap(base_send, "tensor", n_tensor, 1).astype(F32)).astype(BF)
        total = base.astype(F32)
        step = 2
        while step < n_tensor:
            total = total + swap(total.astype(BF), "tensor", n_tensor, step).astype(F32)
            step *= 2

        positions = jnp.arange(rank, dtype=jnp.int32)
        source = ((positions // rank_part) ^ t) * rank_part + positions % rank_part
        reorder = (jnp.arange(rank, dtype=jnp.int32)[:, None] == source[None, :]).astype(BF)
        select = (
            (jnp.arange(owned, dtype=jnp.int32)[:, None] == slot[None, :]) & (owner[None, :] == a)
        ).astype(BF)
        held = jnp.dot(jnp.dot(select, shrunk).astype(BF), reorder).astype(BF)
        in_block = (
            jnp.arange(owned, dtype=jnp.int32)[:, None] // SLOTS
            == jnp.arange(per_owner, dtype=jnp.int32)[None, :]
        )
        wide = jnp.where(in_block[:, :, None], held[:, None, :], 0).reshape(owned, -1)
        terms = jnp.dot(wide.astype(BF), up, preferred_element_type=F32).astype(BF)
        received = []
        for k in range(n_adapter):
            piece = lax.dynamic_slice_in_dim(terms, (a ^ k) * half, half, 1)
            received.append(swap(piece, "adapter", n_adapter, k) if k else piece)
        received = jnp.concatenate(received, axis=0)
        place = (
            ((owner ^ a) * owned + slot)[:, None]
            == jnp.arange(n_adapter * owned, dtype=jnp.int32)[None, :]
        ).astype(BF)
        delta = jnp.dot(place, received, preferred_element_type=F32)
        mine = (total + ADAPTER_SCALE * delta).astype(BF)
        other = swap(mine, "tensor", n_tensor, 1)
        return jnp.where(
            low == 0,
            jnp.concatenate([mine, other], axis=1),
            jnp.concatenate([other, mine], axis=1),
        )

    return shards


def solution(mesh):
    in_specs = (
        P(("groups", "adapter"), "tensor"),
        P(("groups", "adapter"), None, "tensor"),
        P(("groups", "adapter"), None, "tensor"),
        P(("groups", "adapter"), "tensor"),
        P(("groups", "adapter"), "tensor"),
        P(("groups", "adapter")),
        P("groups"),
        P(),
        P("tensor", "adapter"),
        P("adapter", "tensor", None),
        P("adapter", "tensor", None),
    )
    out_specs = P("groups", "adapter")
    sizes = mesh.shape["adapter"], mesh.shape["tensor"]
    fast, plain = make_shards(*sizes), make_plain_shards(*sizes)

    def shards(*arrays):
        return (plain if arrays[8].shape[1] % 256 else fast)(*arrays)

    return jax.shard_map(shards, mesh=mesh, in_specs=in_specs, out_specs=out_specs, check_vma=False)
```

```python
import functools
import math

import jax
import jax.numpy as jnp
from jax import lax
from jax.experimental import pallas as pl
from jax.experimental.pallas import tpu as pltpu
from jax.sharding import PartitionSpec as P

HEAD_SIZE = 128
SLOTS = 32
ADAPTER_SCALE = 2.0
BF = jnp.bfloat16
F32 = jnp.float32
VMEM = pl.BlockSpec(memory_space=pltpu.VMEM)
SMEM = pl.BlockSpec(memory_space=pltpu.SMEM)
ANY = pl.BlockSpec(memory_space=pl.ANY)


def attend_kernel(
    chunk,
    length_ref,
    q_hbm,
    k_hbm,
    v_hbm,
    nk_hbm,
    nv_hbm,
    up_hbm,
    out_ref,
    low_hbm,
    high_hbm,
    q_ref,
    k_ref,
    v_ref,
    nk_ref,
    nv_ref,
    low_ref,
    high_ref,
    sems,
    cut_sems,
    put_sems,
):
    half = low_ref.shape[3]
    low = lax.rem(lax.axis_index("tensor"), 2)
    cuts = []
    for b in range(low_ref.shape[0]):
        for i, (ref, side) in enumerate(((low_ref, low), (high_ref, 1 - low))):
            start = pl.multiple_of((2 * b + side) * half, half)
            cuts.append(
                pltpu.make_async_copy(
                    up_hbm.at[:, :, pl.ds(start, half)], ref.at[b], cut_sems.at[b, i]
                )
            )
    requests, positions, kv_width = k_ref.shape
    heads = q_ref.shape[1] // HEAD_SIZE
    kv_heads = kv_width // HEAD_SIZE
    group = heads // kv_heads
    factor = 1.0 / math.sqrt(HEAD_SIZE)
    extended = positions + chunk

    small = [
        pltpu.make_async_copy(source, target, sems.at[2, i])
        for i, (source, target) in enumerate(((q_hbm, q_ref), (nk_hbm, nk_ref), (nv_hbm, nv_ref)))
    ]
    parts = [pl.ds(first, chunk) for first in range(0, requests, chunk)]
    keys = [
        pltpu.make_async_copy(k_hbm.at[part], k_ref.at[part], sems.at[0, i])
        for i, part in enumerate(parts)
    ]
    values = [
        pltpu.make_async_copy(v_hbm.at[part], v_ref.at[part], sems.at[1, i])
        for i, part in enumerate(parts)
    ]
    for copy in small:
        copy.start()
    for key, value in zip(keys, values):
        key.start()
        value.start()
    for copy in cuts:
        copy.start()

    row_group = lax.broadcasted_iota(jnp.int32, (heads, kv_width), 0) // group
    lane_group = lax.broadcasted_iota(jnp.int32, (heads, kv_width), 1) // HEAD_SIZE
    diagonal = row_group == lane_group
    place = lax.broadcasted_iota(jnp.int32, (heads, extended), 1)
    ones = jnp.ones((extended, HEAD_SIZE), BF)
    for copy in small:
        copy.wait()
    puts = [
        pltpu.make_async_copy(low_ref, low_hbm, put_sems.at[0]),
        pltpu.make_async_copy(high_ref, high_hbm, put_sems.at[1]),
    ]
    for c, first in enumerate(range(0, requests, chunk)):
        if first + chunk >= requests:
            for copy in cuts:
                copy.wait()
            for copy in puts:
                copy.start()
        q = q_ref[first : first + chunk].reshape(chunk, heads, HEAD_SIZE)
        new_keys = nk_ref[first : first + chunk]
        new_values = nv_ref[first : first + chunk]
        keys[c].wait()
        scores = []
        for i in range(chunk):
            r = first + i
            wide = jnp.where(
                diagonal, jnp.concatenate([q[i]] * kv_heads, axis=1), jnp.zeros((), BF)
            )
            score = lax.dot_general(
                wide,
                jnp.concatenate([k_ref[r], new_keys], axis=0),
                (((1,), (1,)), ((), ())),
                preferred_element_type=F32,
            )
            valid = (place < length_ref[r]) | (place == positions + i)
            scores.append(jnp.where(valid, score * factor, -jnp.inf))
        scores = jnp.stack(scores).reshape(chunk * heads, extended)
        powers = jnp.exp(scores - jnp.max(scores, axis=1, keepdims=True)).astype(BF)
        inverse = 1.0 / jnp.dot(powers, ones, preferred_element_type=F32)
        values[c].wait()
        outs = []
        for i in range(chunk):
            rows = slice(i * heads, (i + 1) * heads)
            blend = jnp.dot(
                powers[rows],
                jnp.concatenate([v_ref[first + i], new_values], axis=0),
                preferred_element_type=F32,
            )
            blend = jnp.concatenate(
                [
                    blend[g * group : (g + 1) * group, g * HEAD_SIZE : (g + 1) * HEAD_SIZE]
                    for g in range(kv_heads)
                ],
                axis=0,
            )
            outs.append((blend * inverse[rows]).astype(BF))
        out_ref[first : first + chunk] = jnp.stack(outs).reshape(chunk, heads * HEAD_SIZE)
    for copy in puts:
        copy.wait()


def attend(
    queries, cache_keys, cached_value_rows, new_keys, fresh_value_rows, lengths, up, blocks
):
    requests = queries.shape[0]
    chunk = 16 if requests % 16 == 0 else requests
    per_owner, rank_part, width = up.shape
    part = (blocks, per_owner, rank_part, width // (2 * blocks))
    moved = (queries, cache_keys, cached_value_rows, new_keys, fresh_value_rows)
    return pl.pallas_call(
        functools.partial(attend_kernel, chunk),
        out_shape=[jax.ShapeDtypeStruct(shape, BF) for shape in (queries.shape, part, part)],
        in_specs=[SMEM] + [ANY] * 6,
        out_specs=[VMEM, ANY, ANY],
        scratch_shapes=[pltpu.VMEM(shape, BF) for shape in [x.shape for x in moved] + [part, part]]
        + [
            pltpu.SemaphoreType.DMA((3, max(3, requests // chunk))),
            pltpu.SemaphoreType.DMA((blocks, 2)),
            pltpu.SemaphoreType.DMA((2,)),
        ],
        compiler_params=pltpu.CompilerParams(vmem_limit_bytes=60 << 20),
        cost_estimate=pl.CostEstimate(
            flops=8 * queries.size * cache_keys.shape[1],
            bytes_accessed=4 * cache_keys.size,
            transcendentals=queries.size,
        ),
        name="attend",
    )(lengths, *moved, up)


def blockwise(position, order, size, index):
    moved = jnp.zeros_like(position)
    for i, k in enumerate(order):
        inside = (position >= i * size) & (position < (i + 1) * size)
        moved = jnp.where(inside, position + ((index ^ k) - i) * size, moved)
    return moved


def ids_kernel(order, n_tensor, ids_ref, slots_ref, here_ref, select_ref, place_ref, order_ref):
    tokens, per_owner = here_ref.shape
    owned = select_ref.shape[0]
    rank = order_ref.shape[0]
    a = lax.axis_index("adapter")
    t = lax.axis_index("tensor")
    down = lax.broadcasted_iota(jnp.int32, (tokens, tokens), 0)
    across = lax.broadcasted_iota(jnp.int32, (tokens, tokens), 1)
    ids_row = ids_ref[...].astype(F32)
    ids_column = jnp.sum(jnp.where(down == across, ids_row, 0.0), axis=1, keepdims=True)
    same = ids_row == ids_column

    def stored(ids):
        return sum(
            jnp.where(ids == j, slots_ref[j].astype(F32), 0.0) for j in range(slots_ref.shape[0])
        )

    earlier = jnp.where(same & (across < down), 1.0, 0.0)
    stored_column = stored(ids_column)
    key_column = stored_column * SLOTS + jnp.sum(earlier, axis=1, keepdims=True)
    earlier = jnp.where(same & (down < across), 1.0, 0.0)
    key_row = stored(ids_row) * SLOTS + jnp.sum(earlier, axis=0, keepdims=True)
    key_column, key_row = key_column.astype(jnp.int32), key_row.astype(jnp.int32)
    adapter = lax.broadcasted_iota(jnp.int32, here_ref.shape, 1) + a * per_owner
    here_ref[...] = jnp.where(adapter == stored_column.astype(jnp.int32), 1.0, 0.0)
    slot = lax.broadcasted_iota(jnp.int32, select_ref.shape, 0) + a * owned
    select_ref[...] = jnp.where(slot == key_row, 1.0, 0.0).astype(BF)
    slot = lax.broadcasted_iota(jnp.int32, place_ref.shape, 1)
    slot = blockwise(slot, order, owned, a)
    place_ref[...] = jnp.where(slot == key_column, 1.0, 0.0).astype(BF)
    source = lax.broadcasted_iota(jnp.int32, order_ref.shape, 1)
    source = blockwise(source, range(n_tensor), rank // n_tensor, t)
    target = lax.broadcasted_iota(jnp.int32, order_ref.shape, 0)
    order_ref[...] = jnp.where(source == target, 1.0, 0.0).astype(BF)


def block_rows(k, requests):
    return pl.ds(pl.multiple_of((lax.axis_index("adapter") ^ k) * requests, requests), requests)


def shrink_kernel(order, *refs):
    *blocks, mask_ref, maps_ref, out_ref, total_ref = refs
    requests = blocks[0].shape[0]
    x = jnp.concatenate([b[...] for b in blocks], axis=0)
    mask = jnp.concatenate(
        [mask_ref[block_rows(k, requests), :] for k in order], axis=0
    )
    total = None
    for j in range(maps_ref.shape[0]):
        part = lax.dot_general(x, maps_ref[j], (((1,), (1,)), ((), ())), preferred_element_type=F32)
        part = jnp.where(mask[:, j : j + 1] > 0, part, 0.0)
        total = part if total is None else total + part
    for i, k in enumerate(order):
        total_ref[block_rows(k, requests), :] = total[i * requests : (i + 1) * requests]
    middle = total.shape[0] // 2
    out_ref[...] = jnp.concatenate([total_ref[:middle], total_ref[middle:]], axis=1)


def load_kernel(*refs):
    *pairs, sems = refs
    count = len(pairs) // 2
    copies = [
        pltpu.make_async_copy(source, target, sems.at[i])
        for i, (source, target) in enumerate(zip(pairs[:count], pairs[count:]))
    ]
    for copy in copies:
        copy.start()
    for copy in copies:
        copy.wait()


def project_kernel(other, *refs):
    *blocks, weight_ref, out_ref = refs
    half = out_ref.shape[1]
    tile = 256 if half % 256 == 0 else 128
    side = lax.rem(lax.axis_index("tensor") + other, 2)
    x = jnp.concatenate([b[...] for b in blocks], axis=0)
    for i in range(half // tile):
        start = pl.multiple_of(side * half + i * tile, tile)
        part = jnp.dot(x, weight_ref[:, pl.ds(start, tile)], preferred_element_type=F32)
        out_ref[:, i * tile : (i + 1) * tile] = part.astype(out_ref.dtype)


def join_kernel(keep_ref, came_ref, *out_refs):
    rows = out_refs[0].shape[0]
    for i, out_ref in enumerate(out_refs):
        part = slice(i * rows, (i + 1) * rows)
        out_ref[...] = (keep_ref[part] + came_ref[part].astype(F32)).astype(BF)


def terms_kernel(order, n_parts, *refs):
    n_adapter = len(order)
    parts = refs[:n_parts]
    select_ref, order_ref = refs[n_parts : n_parts + 2]
    maps = refs[n_parts + 2 : -n_adapter]
    outs = refs[-n_adapter:]
    per_owner = maps[0].shape[1]
    a = lax.axis_index("adapter")
    sums = [p[...].astype(F32) for p in parts]
    while len(sums) > 1:
        sums = [x + y for x, y in zip(sums[::2], sums[1::2])]
    rank = sums[0].shape[1] // 2
    shrunk = jnp.concatenate([sums[0][:, :rank], sums[0][:, rank:]], axis=0).astype(BF)
    held = jnp.dot(select_ref[...], shrunk, preferred_element_type=F32)
    held = jnp.dot(held.astype(BF), order_ref[...], preferred_element_type=F32)
    slot_of = lax.broadcasted_iota(jnp.int32, held.shape, 0) // SLOTS
    wide = jnp.concatenate(
        [jnp.where(slot_of == j, held, 0.0) for j in range(per_owner)], axis=1
    ).astype(BF)
    for out, k in zip(outs, order):
        up = jnp.concatenate([m[a ^ k, j] for j in range(per_owner) for m in maps], axis=0)
        out[...] = jnp.dot(wide, up, preferred_element_type=F32).astype(BF)


def finish_kernel(requests, order, place_ref, *refs):
    *base, out_ref = refs
    base, pieces = base[:4], base[4:]
    received = jnp.concatenate([p[...] for p in pieces], axis=0)
    place = jnp.concatenate([place_ref[block_rows(k, requests), :] for k in order], axis=0)
    delta = jnp.dot(place, received, preferred_element_type=F32)
    base = [b[...].astype(F32) for b in base]
    total = jnp.concatenate([base[0] + base[1], base[2] + base[3]], axis=0)
    total = (total + ADAPTER_SCALE * delta).astype(BF)
    for i, k in enumerate(order):
        out_ref[block_rows(k, requests), :] = total[i * requests : (i + 1) * requests]


def make_shards(n_adapter, n_tensor):
    def swap(x, axis, n, k):
        return lax.ppermute(x, axis, [(i, i ^ k) for i in range(n)])

    def shards(
        queries,
        cache_keys,
        cached_value_rows,
        new_keys,
        fresh_value_rows,
        lengths,
        adapter_ids,
        adapter_slots,
        out_weight,
        shrink_weight,
        expand_weight,
    ):
        low = lax.axis_index("tensor") % 2
        per_owner = expand_weight.shape[0]
        rank = shrink_weight.shape[2]
        columns = out_weight.shape[1]
        half = columns // 2
        requests = queries.shape[0]
        tokens = adapter_ids.shape[0]
        owned = per_owner * SLOTS
        order = sorted(range(n_adapter), key=lambda k: (k != 0, k != 2, k))

        attended, up_low, up_high = attend(
            queries,
            cache_keys,
            cached_value_rows,
            new_keys,
            fresh_value_rows,
            lengths,
            expand_weight,
            n_adapter,
        )
        blocks = [swap(attended, "adapter", n_adapter, k) for k in order[1:]]

        maps = [up_low] + [
            swap((up_low, up_high)[k % 2], "tensor", n_tensor, k) for k in range(1, n_tensor)
        ]
        ids = adapter_ids.reshape(1, tokens)
        ids, maps[1] = lax.optimization_barrier((ids, maps[1]))

        here, select, place, reorder = pl.pallas_call(
            functools.partial(ids_kernel, order, n_tensor),
            out_shape=[
                jax.ShapeDtypeStruct((tokens, per_owner), F32),
                jax.ShapeDtypeStruct((owned, tokens), BF),
                jax.ShapeDtypeStruct((tokens, n_adapter * owned), BF),
                jax.ShapeDtypeStruct((rank, rank), BF),
            ],
            in_specs=[VMEM, SMEM],
            out_specs=[VMEM] * 4,
            compiler_params=pltpu.CompilerParams(vmem_limit_bytes=16 << 20),
            name="ids",
        )(ids, adapter_slots)

        out_weight, here = lax.optimization_barrier((out_weight, here))

        loads = (attended, out_weight, jnp.swapaxes(shrink_weight, 1, 2))
        here_block, weight, down = pl.pallas_call(
            load_kernel,
            out_shape=[jax.ShapeDtypeStruct(x.shape, BF) for x in loads],
            in_specs=[ANY] * 3,
            out_specs=[VMEM] * 3,
            scratch_shapes=[pltpu.SemaphoreType.DMA((3,))],
            compiler_params=pltpu.CompilerParams(vmem_limit_bytes=44 << 20),
            cost_estimate=pl.CostEstimate(
                flops=0, bytes_accessed=4 * out_weight.size, transcendentals=0
            ),
            name="load",
        )(*loads)
        blocks = [here_block] + blocks

        shrunk = pl.pallas_call(
            functools.partial(shrink_kernel, order),
            out_shape=jax.ShapeDtypeStruct((tokens // 2, 2 * rank), F32),
            in_specs=[VMEM] * (n_adapter + 2),
            out_specs=VMEM,
            scratch_shapes=[pltpu.VMEM((tokens, rank), F32)],
            compiler_params=pltpu.CompilerParams(vmem_limit_bytes=24 << 20),
            name="shrink",
        )(*blocks, here, down)
        shrunk, *blocks = lax.optimization_barrier((shrunk, *blocks))
        shrunk = (shrunk + swap(shrunk, "tensor", n_tensor, 1)).astype(BF)
        shrunk = [shrunk] + [swap(shrunk, "tensor", n_tensor, k) for k in range(2, n_tensor, 2)]


        def project(other, dtype):
            return pl.pallas_call(
                functools.partial(project_kernel, other),
                out_shape=jax.ShapeDtypeStruct((tokens, half), dtype),
                in_specs=[VMEM] * (n_adapter + 1),
                out_specs=VMEM,
                compiler_params=pltpu.CompilerParams(vmem_limit_bytes=24 << 20),
                cost_estimate=pl.CostEstimate(
                    flops=tokens * out_weight.size,
                    bytes_accessed=2 * out_weight.size,
                    transcendentals=0,
                ),
                name="project",
            )(*blocks, weight)

        came = swap(project(1, BF), "tensor", n_tensor, 1)
        base = pl.pallas_call(
            join_kernel,
            out_shape=[jax.ShapeDtypeStruct((tokens // 2, half), BF)] * 2,
            in_specs=[VMEM] * 2,
            out_specs=[VMEM] * 2,
            compiler_params=pltpu.CompilerParams(vmem_limit_bytes=16 << 20),
            name="join",
        )(project(0, F32), came)
        base = list(lax.optimization_barrier((*base, *shrunk)))
        base, shrunk = base[:2], base[2:]

        terms = pl.pallas_call(
            functools.partial(terms_kernel, order, len(shrunk)),
            out_shape=[jax.ShapeDtypeStruct((owned, half), BF)] * n_adapter,
            in_specs=[VMEM] * (2 + len(shrunk) + len(maps)),
            out_specs=[VMEM] * n_adapter,
            compiler_params=pltpu.CompilerParams(vmem_limit_bytes=24 << 20),
            name="terms",
        )(*shrunk, select, reorder, *maps)
        received = [terms[0]] + [
            swap(term, "adapter", n_adapter, k) for term, k in zip(terms[1:], order[1:])
        ]

        sums = []
        for part in base:
            step = 2
            while step * 2 < n_tensor:
                other = swap(part, "tensor", n_tensor, step)
                part = (part.astype(F32) + other.astype(F32)).astype(BF)
                step *= 2
            sums += [part, swap(part, "tensor", n_tensor, step)]

        mine = pl.pallas_call(
            functools.partial(finish_kernel, requests, order),
            out_shape=jax.ShapeDtypeStruct((tokens, half), BF),
            in_specs=[VMEM] * (5 + n_adapter),
            out_specs=VMEM,
            compiler_params=pltpu.CompilerParams(vmem_limit_bytes=24 << 20),
            name="finish",
        )(place, *sums, *received)
        other = swap(mine, "tensor", n_tensor, 1)
        return jnp.where(
            low == 0,
            jnp.concatenate([mine, other], axis=1),
            jnp.concatenate([other, mine], axis=1),
        )

    return shards


def plain_attend(queries, cache_keys, cached_value_rows, new_keys, fresh_value_rows, lengths):
    requests = queries.shape[0]
    positions = cache_keys.shape[1]
    kv_local = cache_keys.shape[2] // HEAD_SIZE
    heads_local = queries.shape[1] // HEAD_SIZE
    group_size = heads_local // kv_local
    factor_term = 1.0 / math.sqrt(HEAD_SIZE)
    q = queries.reshape(requests, kv_local, group_size, HEAD_SIZE)
    k = cache_keys.reshape(requests, positions, kv_local, HEAD_SIZE)
    v = cached_value_rows.reshape(requests, positions, kv_local, HEAD_SIZE)
    scores = jnp.einsum("rkgd,rckd->rkgc", q, k, preferred_element_type=F32) * factor_term
    own = (
        jnp.einsum(
            "ivhz,ivz->ivh",
            q,
            new_keys.reshape(requests, kv_local, HEAD_SIZE),
            preferred_element_type=F32,
        )
        * factor_term
    )
    valid = jnp.arange(positions)[None, None, None, :] < lengths[:, None, None, None]
    scores = jnp.where(valid, scores, -jnp.inf)
    row_top = jnp.maximum(jnp.max(scores, axis=-1), own)
    powers = jnp.exp(scores - row_top[..., None])
    own_power = jnp.exp(own - row_top)
    row_total = jnp.sum(powers, axis=-1) + own_power
    weights = (powers / row_total[..., None]).astype(BF)
    own_weight = (own_power / row_total).astype(BF)
    blended = jnp.einsum("rkgc,rckd->rkgd", weights, v, preferred_element_type=F32)
    blended = blended + own_weight.astype(F32)[..., None] * fresh_value_rows.reshape(
        requests, kv_local, 1, HEAD_SIZE
    ).astype(F32)
    return blended.reshape(requests, heads_local * HEAD_SIZE).astype(BF)


def make_plain_shards(n_adapter, n_tensor):
    def swap(x, axis, n, k):
        return lax.ppermute(x, axis, [(i, i ^ k) for i in range(n)])

    def shards(
        queries,
        cache_keys,
        cached_value_rows,
        new_keys,
        fresh_value_rows,
        lengths,
        adapter_ids,
        adapter_slots,
        out_weight,
        shrink_weight,
        expand_weight,
    ):
        a = lax.axis_index("adapter")
        t = lax.axis_index("tensor")
        low = t % 2
        adapters = adapter_slots.shape[0]
        per_owner, rank_part, width = expand_weight.shape
        rank = shrink_weight.shape[2]
        columns = out_weight.shape[1]
        half = columns // 2
        requests = queries.shape[0]
        tokens = adapter_ids.shape[0]
        owned = per_owner * SLOTS

        up = expand_weight.reshape(per_owner, rank_part, n_adapter, 2, half)
        up_keep = lax.dynamic_index_in_dim(up, low, 3, keepdims=False)
        up_send = lax.dynamic_index_in_dim(up, 1 - low, 3, keepdims=False)
        up = jnp.concatenate([up_keep, swap(up_send, "tensor", n_tensor, 1)], axis=1)
        step = 2
        while step < n_tensor:
            up = jnp.concatenate([up, swap(up, "tensor", n_tensor, step)], axis=1)
            step *= 2
        up = up.reshape(per_owner * rank, n_adapter * half)

        attended = plain_attend(
            queries, cache_keys, cached_value_rows, new_keys, fresh_value_rows, lengths
        )

        matches = adapter_ids[:, None] == jnp.arange(adapters, dtype=jnp.int32)[None, :]
        counts = matches.astype(jnp.int32)
        rank_within = jnp.sum(jnp.cumsum(counts, axis=0) * counts, axis=1) - 1
        stored = jnp.sum(counts * adapter_slots[None, :], axis=1)
        owner = stored // per_owner
        slot = (stored % per_owner) * SLOTS + rank_within

        blocks = [attended] + [swap(attended, "adapter", n_adapter, k) for k in range(1, n_adapter)]
        rows = jnp.zeros((tokens, queries.shape[1]), BF)
        for k, block in enumerate(blocks):
            rows = lax.dynamic_update_slice(rows, block, ((a ^ k) * requests, 0))

        parts = jnp.einsum("rd,adn->arn", rows, shrink_weight, preferred_element_type=F32)
        here = stored[None, :] - a * per_owner == jnp.arange(per_owner, dtype=jnp.int32)[:, None]
        shrunk = jnp.sum(jnp.where(here[:, :, None], parts, 0.0), axis=0)
        step = 1
        while step < n_tensor:
            shrunk = shrunk + swap(shrunk, "tensor", n_tensor, step)
            step *= 2
        shrunk = shrunk.astype(BF)

        base = jnp.dot(rows, out_weight, preferred_element_type=F32)
        base_keep = lax.dynamic_slice_in_dim(base, low * half, half, 1)
        base_send = lax.dynamic_slice_in_dim(base, (1 - low) * half, half, 1).astype(BF)
        base = (base_keep + swap(base_send, "tensor", n_tensor, 1).astype(F32)).astype(BF)
        total = base.astype(F32)
        step = 2
        while step < n_tensor:
            total = total + swap(total.astype(BF), "tensor", n_tensor, step).astype(F32)
            step *= 2

        positions = jnp.arange(rank, dtype=jnp.int32)
        source = ((positions // rank_part) ^ t) * rank_part + positions % rank_part
        reorder = (jnp.arange(rank, dtype=jnp.int32)[:, None] == source[None, :]).astype(BF)
        select = (
            (jnp.arange(owned, dtype=jnp.int32)[:, None] == slot[None, :]) & (owner[None, :] == a)
        ).astype(BF)
        held = jnp.dot(jnp.dot(select, shrunk).astype(BF), reorder).astype(BF)
        in_block = (
            jnp.arange(owned, dtype=jnp.int32)[:, None] // SLOTS
            == jnp.arange(per_owner, dtype=jnp.int32)[None, :]
        )
        wide = jnp.where(in_block[:, :, None], held[:, None, :], 0).reshape(owned, -1)
        terms = jnp.dot(wide.astype(BF), up, preferred_element_type=F32).astype(BF)
        received = []
        for k in range(n_adapter):
            piece = lax.dynamic_slice_in_dim(terms, (a ^ k) * half, half, 1)
            received.append(swap(piece, "adapter", n_adapter, k) if k else piece)
        received = jnp.concatenate(received, axis=0)
        place = (
            ((owner ^ a) * owned + slot)[:, None]
            == jnp.arange(n_adapter * owned, dtype=jnp.int32)[None, :]
        ).astype(BF)
        delta = jnp.dot(place, received, preferred_element_type=F32)
        mine = (total + ADAPTER_SCALE * delta).astype(BF)
        other = swap(mine, "tensor", n_tensor, 1)
        return jnp.where(
            low == 0,
            jnp.concatenate([mine, other], axis=1),
            jnp.concatenate([other, mine], axis=1),
        )

    return shards


def solution(mesh):
    in_specs = (
        P(("groups", "adapter"), "tensor"),
        P(("groups", "adapter"), None, "tensor"),
        P(("groups", "adapter"), None, "tensor"),
        P(("groups", "adapter"), "tensor"),
        P(("groups", "adapter"), "tensor"),
        P(("groups", "adapter")),
        P("groups"),
        P(),
        P("tensor", "adapter"),
        P("adapter", "tensor", None),
        P("adapter", "tensor", None),
    )
    out_specs = P("groups", "adapter")
    sizes = mesh.shape["adapter"], mesh.shape["tensor"]
    fast, plain = make_shards(*sizes), make_plain_shards(*sizes)

    def shards(*arrays):
        return (plain if arrays[8].shape[1] % 256 else fast)(*arrays)

    return jax.shard_map(shards, mesh=mesh, in_specs=in_specs, out_specs=out_specs, check_vma=False)
```

```python
import functools
import math

import jax
import jax.numpy as jnp
from jax import lax
from jax.experimental import pallas as pl
from jax.experimental.pallas import tpu as pltpu
from jax.sharding import PartitionSpec as P

HEAD_SIZE = 128
SLOTS = 32
ADAPTER_SCALE = 2.0
BF = jnp.bfloat16
F32 = jnp.float32
VMEM = pl.BlockSpec(memory_space=pltpu.VMEM)
SMEM = pl.BlockSpec(memory_space=pltpu.SMEM)
ANY = pl.BlockSpec(memory_space=pl.ANY)


def attend_kernel(
    chunk,
    length_ref,
    q_hbm,
    k_hbm,
    v_hbm,
    nk_hbm,
    nv_hbm,
    up_hbm,
    out_ref,
    low_hbm,
    high_hbm,
    q_ref,
    k_ref,
    v_ref,
    nk_ref,
    nv_ref,
    low_ref,
    high_ref,
    sems,
    cut_sems,
    put_sems,
):
    half = low_ref.shape[3]
    low = lax.rem(lax.axis_index("tensor"), 2)
    cuts = []
    for b in range(low_ref.shape[0]):
        for i, (ref, side) in enumerate(((low_ref, low), (high_ref, 1 - low))):
            start = pl.multiple_of((2 * b + side) * half, half)
            cuts.append(
                pltpu.make_async_copy(
                    up_hbm.at[:, :, pl.ds(start, half)], ref.at[b], cut_sems.at[b, i]
                )
            )
    requests, positions, kv_width = k_ref.shape
    heads = q_ref.shape[1] // HEAD_SIZE
    kv_heads = kv_width // HEAD_SIZE
    group = heads // kv_heads
    factor = 1.0 / math.sqrt(HEAD_SIZE)
    extended = positions + chunk

    small = [
        pltpu.make_async_copy(source, target, sems.at[2, i])
        for i, (source, target) in enumerate(((q_hbm, q_ref), (nk_hbm, nk_ref), (nv_hbm, nv_ref)))
    ]
    parts = [pl.ds(first, chunk) for first in range(0, requests, chunk)]
    keys = [
        pltpu.make_async_copy(k_hbm.at[part], k_ref.at[part], sems.at[0, i])
        for i, part in enumerate(parts)
    ]
    values = [
        pltpu.make_async_copy(v_hbm.at[part], v_ref.at[part], sems.at[1, i])
        for i, part in enumerate(parts)
    ]
    keys[0].start()
    for copy in small:
        copy.start()
    for copy in keys[1:] + values:
        copy.start()
    for copy in cuts:
        copy.start()

    row_group = lax.broadcasted_iota(jnp.int32, (heads, kv_width), 0) // group
    lane_group = lax.broadcasted_iota(jnp.int32, (heads, kv_width), 1) // HEAD_SIZE
    diagonal = row_group == lane_group
    place = lax.broadcasted_iota(jnp.int32, (heads, extended), 1)
    ones = jnp.ones((extended, HEAD_SIZE), BF)
    for copy in small:
        copy.wait()
    puts = [
        pltpu.make_async_copy(low_ref, low_hbm, put_sems.at[0]),
        pltpu.make_async_copy(high_ref, high_hbm, put_sems.at[1]),
    ]
    for c, first in enumerate(range(0, requests, chunk)):
        q = q_ref[first : first + chunk].reshape(chunk, heads, HEAD_SIZE)
        new_keys = nk_ref[first : first + chunk]
        new_values = nv_ref[first : first + chunk]
        keys[c].wait()
        scores = []
        for i in range(chunk):
            r = first + i
            wide = jnp.where(
                diagonal, jnp.concatenate([q[i]] * kv_heads, axis=1), jnp.zeros((), BF)
            )
            score = lax.dot_general(
                wide,
                jnp.concatenate([k_ref[r], new_keys], axis=0),
                (((1,), (1,)), ((), ())),
                preferred_element_type=F32,
            )
            valid = (place < length_ref[r]) | (place == positions + i)
            scores.append(jnp.where(valid, score * factor, -jnp.inf))
        scores = jnp.stack(scores).reshape(chunk * heads, extended)
        powers = jnp.exp(scores - jnp.max(scores, axis=1, keepdims=True)).astype(BF)
        inverse = 1.0 / jnp.dot(powers, ones, preferred_element_type=F32)
        if c == 0:
            for copy in cuts:
                copy.wait()
            for copy in puts:
                copy.start()
        values[c].wait()
        outs = []
        for i in range(chunk):
            rows = slice(i * heads, (i + 1) * heads)
            blend = jnp.dot(
                powers[rows],
                jnp.concatenate([v_ref[first + i], new_values], axis=0),
                preferred_element_type=F32,
            )
            blend = jnp.concatenate(
                [
                    blend[g * group : (g + 1) * group, g * HEAD_SIZE : (g + 1) * HEAD_SIZE]
                    for g in range(kv_heads)
                ],
                axis=0,
            )
            outs.append((blend * inverse[rows]).astype(BF))
        out_ref[first : first + chunk] = jnp.stack(outs).reshape(chunk, heads * HEAD_SIZE)
    for copy in puts:
        copy.wait()


def attend(
    queries, cache_keys, cached_value_rows, new_keys, fresh_value_rows, lengths, up, blocks
):
    requests = queries.shape[0]
    chunk = 16 if requests % 16 == 0 else requests
    per_owner, rank_part, width = up.shape
    part = (blocks, per_owner, rank_part, width // (2 * blocks))
    moved = (queries, cache_keys, cached_value_rows, new_keys, fresh_value_rows)
    return pl.pallas_call(
        functools.partial(attend_kernel, chunk),
        out_shape=[jax.ShapeDtypeStruct(shape, BF) for shape in (queries.shape, part, part)],
        in_specs=[SMEM] + [ANY] * 6,
        out_specs=[VMEM, ANY, ANY],
        scratch_shapes=[pltpu.VMEM(shape, BF) for shape in [x.shape for x in moved] + [part, part]]
        + [
            pltpu.SemaphoreType.DMA((3, max(3, requests // chunk))),
            pltpu.SemaphoreType.DMA((blocks, 2)),
            pltpu.SemaphoreType.DMA((2,)),
        ],
        compiler_params=pltpu.CompilerParams(vmem_limit_bytes=60 << 20),
        cost_estimate=pl.CostEstimate(
            flops=8 * queries.size * cache_keys.shape[1],
            bytes_accessed=4 * cache_keys.size,
            transcendentals=queries.size,
        ),
        name="attend",
    )(lengths, *moved, up)


def blockwise(position, order, size, index):
    moved = jnp.zeros_like(position)
    for i, k in enumerate(order):
        inside = (position >= i * size) & (position < (i + 1) * size)
        moved = jnp.where(inside, position + ((index ^ k) - i) * size, moved)
    return moved


def ids_kernel(order, n_tensor, ids_ref, slots_ref, here_ref, select_ref, place_ref, order_ref):
    tokens, per_owner = here_ref.shape
    owned = select_ref.shape[0]
    rank = order_ref.shape[0]
    a = lax.axis_index("adapter")
    t = lax.axis_index("tensor")
    down = lax.broadcasted_iota(jnp.int32, (tokens, tokens), 0)
    across = lax.broadcasted_iota(jnp.int32, (tokens, tokens), 1)
    ids_row = ids_ref[...].astype(F32)
    ids_column = jnp.sum(jnp.where(down == across, ids_row, 0.0), axis=1, keepdims=True)
    same = ids_row == ids_column

    def stored(ids):
        return sum(
            jnp.where(ids == j, slots_ref[j].astype(F32), 0.0) for j in range(slots_ref.shape[0])
        )

    earlier = jnp.where(same & (across < down), 1.0, 0.0)
    stored_column = stored(ids_column)
    key_column = stored_column * SLOTS + jnp.sum(earlier, axis=1, keepdims=True)
    earlier = jnp.where(same & (down < across), 1.0, 0.0)
    key_row = stored(ids_row) * SLOTS + jnp.sum(earlier, axis=0, keepdims=True)
    key_column, key_row = key_column.astype(jnp.int32), key_row.astype(jnp.int32)
    adapter = lax.broadcasted_iota(jnp.int32, here_ref.shape, 1) + a * per_owner
    here_ref[...] = jnp.where(adapter == stored_column.astype(jnp.int32), 1.0, 0.0)
    slot = lax.broadcasted_iota(jnp.int32, select_ref.shape, 0) + a * owned
    select_ref[...] = jnp.where(slot == key_row, 1.0, 0.0).astype(BF)
    slot = lax.broadcasted_iota(jnp.int32, place_ref.shape, 1)
    slot = blockwise(slot, order, owned, a)
    place_ref[...] = jnp.where(slot == key_column, 1.0, 0.0).astype(BF)
    source = lax.broadcasted_iota(jnp.int32, order_ref.shape, 1)
    source = blockwise(source, range(n_tensor), rank // n_tensor, t)
    target = lax.broadcasted_iota(jnp.int32, order_ref.shape, 0)
    order_ref[...] = jnp.where(source == target, 1.0, 0.0).astype(BF)


def block_rows(k, requests):
    return pl.ds(pl.multiple_of((lax.axis_index("adapter") ^ k) * requests, requests), requests)


def shrink_kernel(order, *refs):
    *blocks, mask_ref, maps_ref, out_ref, total_ref = refs
    requests = blocks[0].shape[0]
    x = jnp.concatenate([b[...] for b in blocks], axis=0)
    mask = jnp.concatenate(
        [mask_ref[block_rows(k, requests), :] for k in order], axis=0
    )
    total = None
    for j in range(maps_ref.shape[0]):
        part = lax.dot_general(x, maps_ref[j], (((1,), (1,)), ((), ())), preferred_element_type=F32)
        part = jnp.where(mask[:, j : j + 1] > 0, part, 0.0)
        total = part if total is None else total + part
    for i, k in enumerate(order):
        total_ref[block_rows(k, requests), :] = total[i * requests : (i + 1) * requests]
    middle = total.shape[0] // 2
    out_ref[...] = jnp.concatenate([total_ref[:middle], total_ref[middle:]], axis=1)


def load_kernel(*refs):
    *pairs, sems = refs
    count = len(pairs) // 2
    copies = [
        pltpu.make_async_copy(source, target, sems.at[i])
        for i, (source, target) in enumerate(zip(pairs[:count], pairs[count:]))
    ]
    for copy in copies:
        copy.start()
    for copy in copies:
        copy.wait()


def project_kernel(other, *refs):
    *blocks, weight_ref, out_ref = refs
    half = out_ref.shape[1]
    tile = 256 if half % 256 == 0 else 128
    side = lax.rem(lax.axis_index("tensor") + other, 2)
    x = jnp.concatenate([b[...] for b in blocks], axis=0)
    for i in range(half // tile):
        start = pl.multiple_of(side * half + i * tile, tile)
        part = jnp.dot(x, weight_ref[:, pl.ds(start, tile)], preferred_element_type=F32)
        out_ref[:, i * tile : (i + 1) * tile] = part.astype(out_ref.dtype)


def join_kernel(keep_ref, came_ref, *out_refs):
    rows = out_refs[0].shape[0]
    for i, out_ref in enumerate(out_refs):
        part = slice(i * rows, (i + 1) * rows)
        out_ref[...] = (keep_ref[part] + came_ref[part].astype(F32)).astype(BF)


def terms_kernel(order, n_parts, *refs):
    n_adapter = len(order)
    parts = refs[:n_parts]
    select_ref, order_ref = refs[n_parts : n_parts + 2]
    maps = refs[n_parts + 2 : -n_adapter]
    outs = refs[-n_adapter:]
    per_owner = maps[0].shape[1]
    a = lax.axis_index("adapter")
    sums = [p[...].astype(F32) for p in parts]
    while len(sums) > 1:
        sums = [x + y for x, y in zip(sums[::2], sums[1::2])]
    rank = sums[0].shape[1] // 2
    shrunk = jnp.concatenate([sums[0][:, :rank], sums[0][:, rank:]], axis=0).astype(BF)
    held = jnp.dot(select_ref[...], shrunk, preferred_element_type=F32)
    held = jnp.dot(held.astype(BF), order_ref[...], preferred_element_type=F32)
    slot_of = lax.broadcasted_iota(jnp.int32, held.shape, 0) // SLOTS
    wide = jnp.concatenate(
        [jnp.where(slot_of == j, held, 0.0) for j in range(per_owner)], axis=1
    ).astype(BF)
    for out, k in zip(outs, order):
        up = jnp.concatenate([m[a ^ k, j] for j in range(per_owner) for m in maps], axis=0)
        out[...] = jnp.dot(wide, up, preferred_element_type=F32).astype(BF)


def finish_kernel(requests, order, place_ref, *refs):
    *base, out_ref = refs
    base, pieces = base[:4], base[4:]
    received = jnp.concatenate([p[...] for p in pieces], axis=0)
    place = jnp.concatenate([place_ref[block_rows(k, requests), :] for k in order], axis=0)
    delta = jnp.dot(place, received, preferred_element_type=F32)
    base = [b[...].astype(F32) for b in base]
    total = jnp.concatenate([base[0] + base[1], base[2] + base[3]], axis=0)
    total = (total + ADAPTER_SCALE * delta).astype(BF)
    for i, k in enumerate(order):
        out_ref[block_rows(k, requests), :] = total[i * requests : (i + 1) * requests]


def beside_kernel(mine_ref, other_ref, out_ref):
    own = pl.program_id(0) == lax.rem(lax.axis_index("tensor"), 2)

    @pl.when(own)
    def _():
        out_ref[...] = mine_ref[...]

    @pl.when(jnp.logical_not(own))
    def _():
        out_ref[...] = other_ref[...]


def make_shards(n_adapter, n_tensor):
    def swap(x, axis, n, k):
        return lax.ppermute(x, axis, [(i, i ^ k) for i in range(n)])

    def shards(
        queries,
        cache_keys,
        cached_value_rows,
        new_keys,
        fresh_value_rows,
        lengths,
        adapter_ids,
        adapter_slots,
        out_weight,
        shrink_weight,
        expand_weight,
    ):
        per_owner = expand_weight.shape[0]
        rank = shrink_weight.shape[2]
        columns = out_weight.shape[1]
        half = columns // 2
        requests = queries.shape[0]
        tokens = adapter_ids.shape[0]
        owned = per_owner * SLOTS
        order = sorted(range(n_adapter), key=lambda k: (k != 0, k != 2, k))

        attended, up_low, up_high = attend(
            queries,
            cache_keys,
            cached_value_rows,
            new_keys,
            fresh_value_rows,
            lengths,
            expand_weight,
            n_adapter,
        )
        blocks = [swap(attended, "adapter", n_adapter, k) for k in order[1:]]

        maps = [up_low] + [
            swap((up_low, up_high)[k % 2], "tensor", n_tensor, k) for k in range(1, n_tensor)
        ]
        ids = adapter_ids.reshape(1, tokens)
        ids, maps[1] = lax.optimization_barrier((ids, maps[1]))

        here, select, place, reorder = pl.pallas_call(
            functools.partial(ids_kernel, order, n_tensor),
            out_shape=[
                jax.ShapeDtypeStruct((tokens, per_owner), F32),
                jax.ShapeDtypeStruct((owned, tokens), BF),
                jax.ShapeDtypeStruct((tokens, n_adapter * owned), BF),
                jax.ShapeDtypeStruct((rank, rank), BF),
            ],
            in_specs=[VMEM, SMEM],
            out_specs=[VMEM] * 4,
            compiler_params=pltpu.CompilerParams(vmem_limit_bytes=16 << 20),
            name="ids",
        )(ids, adapter_slots)

        out_weight, here = lax.optimization_barrier((out_weight, here))

        loads = (attended, out_weight, jnp.swapaxes(shrink_weight, 1, 2))
        here_block, weight, down = pl.pallas_call(
            load_kernel,
            out_shape=[jax.ShapeDtypeStruct(x.shape, BF) for x in loads],
            in_specs=[ANY] * 3,
            out_specs=[VMEM] * 3,
            scratch_shapes=[pltpu.SemaphoreType.DMA((3,))],
            compiler_params=pltpu.CompilerParams(vmem_limit_bytes=44 << 20),
            cost_estimate=pl.CostEstimate(
                flops=0, bytes_accessed=4 * out_weight.size, transcendentals=0
            ),
            name="load",
        )(*loads)
        blocks = [here_block] + blocks

        shrunk = pl.pallas_call(
            functools.partial(shrink_kernel, order),
            out_shape=jax.ShapeDtypeStruct((tokens // 2, 2 * rank), F32),
            in_specs=[VMEM] * (n_adapter + 2),
            out_specs=VMEM,
            scratch_shapes=[pltpu.VMEM((tokens, rank), F32)],
            compiler_params=pltpu.CompilerParams(vmem_limit_bytes=24 << 20),
            name="shrink",
        )(*blocks, here, down)
        shrunk, *blocks = lax.optimization_barrier((shrunk, *blocks))
        shrunk = (shrunk + swap(shrunk, "tensor", n_tensor, 1)).astype(BF)
        shrunk = [shrunk] + [swap(shrunk, "tensor", n_tensor, k) for k in range(2, n_tensor, 2)]


        def project(other, dtype):
            return pl.pallas_call(
                functools.partial(project_kernel, other),
                out_shape=jax.ShapeDtypeStruct((tokens, half), dtype),
                in_specs=[VMEM] * (n_adapter + 1),
                out_specs=VMEM,
                compiler_params=pltpu.CompilerParams(vmem_limit_bytes=24 << 20),
                cost_estimate=pl.CostEstimate(
                    flops=tokens * out_weight.size,
                    bytes_accessed=2 * out_weight.size,
                    transcendentals=0,
                ),
                name="project",
            )(*blocks, weight)

        came = swap(project(1, BF), "tensor", n_tensor, 1)
        base = pl.pallas_call(
            join_kernel,
            out_shape=[jax.ShapeDtypeStruct((tokens // 2, half), BF)] * 2,
            in_specs=[VMEM] * 2,
            out_specs=[VMEM] * 2,
            compiler_params=pltpu.CompilerParams(vmem_limit_bytes=16 << 20),
            name="join",
        )(project(0, F32), came)
        base = list(lax.optimization_barrier((*base, *shrunk)))
        base, shrunk = base[:2], base[2:]

        terms = pl.pallas_call(
            functools.partial(terms_kernel, order, len(shrunk)),
            out_shape=[jax.ShapeDtypeStruct((owned, half), BF)] * n_adapter,
            in_specs=[VMEM] * (2 + len(shrunk) + len(maps)),
            out_specs=[VMEM] * n_adapter,
            compiler_params=pltpu.CompilerParams(vmem_limit_bytes=24 << 20),
            name="terms",
        )(*shrunk, select, reorder, *maps)
        received = [terms[0]] + [
            swap(term, "adapter", n_adapter, k) for term, k in zip(terms[1:], order[1:])
        ]

        sums = []
        for part in base:
            step = 2
            while step * 2 < n_tensor:
                other = swap(part, "tensor", n_tensor, step)
                part = (part.astype(F32) + other.astype(F32)).astype(BF)
                step *= 2
            sums += [part, swap(part, "tensor", n_tensor, step)]

        mine = pl.pallas_call(
            functools.partial(finish_kernel, requests, order),
            out_shape=jax.ShapeDtypeStruct((tokens, half), BF),
            in_specs=[VMEM] * (5 + n_adapter),
            out_specs=VMEM,
            compiler_params=pltpu.CompilerParams(vmem_limit_bytes=24 << 20),
            name="finish",
        )(place, *sums, *received)
        other = swap(mine, "tensor", n_tensor, 1)
        return pl.pallas_call(
            beside_kernel,
            out_shape=jax.ShapeDtypeStruct((tokens, columns), BF),
            grid=(2,),
            in_specs=[VMEM] * 2,
            out_specs=pl.BlockSpec((tokens, half), lambda i: (0, i)),
            compiler_params=pltpu.CompilerParams(vmem_limit_bytes=16 << 20),
            name="beside",
        )(mine, other)

    return shards


def plain_attend(queries, cache_keys, cached_value_rows, new_keys, fresh_value_rows, lengths):
    requests = queries.shape[0]
    positions = cache_keys.shape[1]
    kv_local = cache_keys.shape[2] // HEAD_SIZE
    heads_local = queries.shape[1] // HEAD_SIZE
    group_size = heads_local // kv_local
    factor_term = 1.0 / math.sqrt(HEAD_SIZE)
    q = queries.reshape(requests, kv_local, group_size, HEAD_SIZE)
    k = cache_keys.reshape(requests, positions, kv_local, HEAD_SIZE)
    v = cached_value_rows.reshape(requests, positions, kv_local, HEAD_SIZE)
    scores = jnp.einsum("rkgd,rckd->rkgc", q, k, preferred_element_type=F32) * factor_term
    own = (
        jnp.einsum(
            "ivhz,ivz->ivh",
            q,
            new_keys.reshape(requests, kv_local, HEAD_SIZE),
            preferred_element_type=F32,
        )
        * factor_term
    )
    valid = jnp.arange(positions)[None, None, None, :] < lengths[:, None, None, None]
    scores = jnp.where(valid, scores, -jnp.inf)
    row_top = jnp.maximum(jnp.max(scores, axis=-1), own)
    powers = jnp.exp(scores - row_top[..., None])
    own_power = jnp.exp(own - row_top)
    row_total = jnp.sum(powers, axis=-1) + own_power
    weights = (powers / row_total[..., None]).astype(BF)
    own_weight = (own_power / row_total).astype(BF)
    blended = jnp.einsum("rkgc,rckd->rkgd", weights, v, preferred_element_type=F32)
    blended = blended + own_weight.astype(F32)[..., None] * fresh_value_rows.reshape(
        requests, kv_local, 1, HEAD_SIZE
    ).astype(F32)
    return blended.reshape(requests, heads_local * HEAD_SIZE).astype(BF)


def make_plain_shards(n_adapter, n_tensor):
    def swap(x, axis, n, k):
        return lax.ppermute(x, axis, [(i, i ^ k) for i in range(n)])

    def shards(
        queries,
        cache_keys,
        cached_value_rows,
        new_keys,
        fresh_value_rows,
        lengths,
        adapter_ids,
        adapter_slots,
        out_weight,
        shrink_weight,
        expand_weight,
    ):
        a = lax.axis_index("adapter")
        t = lax.axis_index("tensor")
        low = t % 2
        adapters = adapter_slots.shape[0]
        per_owner, rank_part, width = expand_weight.shape
        rank = shrink_weight.shape[2]
        columns = out_weight.shape[1]
        half = columns // 2
        requests = queries.shape[0]
        tokens = adapter_ids.shape[0]
        owned = per_owner * SLOTS

        up = expand_weight.reshape(per_owner, rank_part, n_adapter, 2, half)
        up_keep = lax.dynamic_index_in_dim(up, low, 3, keepdims=False)
        up_send = lax.dynamic_index_in_dim(up, 1 - low, 3, keepdims=False)
        up = jnp.concatenate([up_keep, swap(up_send, "tensor", n_tensor, 1)], axis=1)
        step = 2
        while step < n_tensor:
            up = jnp.concatenate([up, swap(up, "tensor", n_tensor, step)], axis=1)
            step *= 2
        up = up.reshape(per_owner * rank, n_adapter * half)

        attended = plain_attend(
            queries, cache_keys, cached_value_rows, new_keys, fresh_value_rows, lengths
        )

        matches = adapter_ids[:, None] == jnp.arange(adapters, dtype=jnp.int32)[None, :]
        counts = matches.astype(jnp.int32)
        rank_within = jnp.sum(jnp.cumsum(counts, axis=0) * counts, axis=1) - 1
        stored = jnp.sum(counts * adapter_slots[None, :], axis=1)
        owner = stored // per_owner
        slot = (stored % per_owner) * SLOTS + rank_within

        blocks = [attended] + [swap(attended, "adapter", n_adapter, k) for k in range(1, n_adapter)]
        rows = jnp.zeros((tokens, queries.shape[1]), BF)
        for k, block in enumerate(blocks):
            rows = lax.dynamic_update_slice(rows, block, ((a ^ k) * requests, 0))

        parts = jnp.einsum("rd,adn->arn", rows, shrink_weight, preferred_element_type=F32)
        here = stored[None, :] - a * per_owner == jnp.arange(per_owner, dtype=jnp.int32)[:, None]
        shrunk = jnp.sum(jnp.where(here[:, :, None], parts, 0.0), axis=0)
        step = 1
        while step < n_tensor:
            shrunk = shrunk + swap(shrunk, "tensor", n_tensor, step)
            step *= 2
        shrunk = shrunk.astype(BF)

        base = jnp.dot(rows, out_weight, preferred_element_type=F32)
        base_keep = lax.dynamic_slice_in_dim(base, low * half, half, 1)
        base_send = lax.dynamic_slice_in_dim(base, (1 - low) * half, half, 1).astype(BF)
        base = (base_keep + swap(base_send, "tensor", n_tensor, 1).astype(F32)).astype(BF)
        total = base.astype(F32)
        step = 2
        while step < n_tensor:
            total = total + swap(total.astype(BF), "tensor", n_tensor, step).astype(F32)
            step *= 2

        positions = jnp.arange(rank, dtype=jnp.int32)
        source = ((positions // rank_part) ^ t) * rank_part + positions % rank_part
        reorder = (jnp.arange(rank, dtype=jnp.int32)[:, None] == source[None, :]).astype(BF)
        select = (
            (jnp.arange(owned, dtype=jnp.int32)[:, None] == slot[None, :]) & (owner[None, :] == a)
        ).astype(BF)
        held = jnp.dot(jnp.dot(select, shrunk).astype(BF), reorder).astype(BF)
        in_block = (
            jnp.arange(owned, dtype=jnp.int32)[:, None] // SLOTS
            == jnp.arange(per_owner, dtype=jnp.int32)[None, :]
        )
        wide = jnp.where(in_block[:, :, None], held[:, None, :], 0).reshape(owned, -1)
        terms = jnp.dot(wide.astype(BF), up, preferred_element_type=F32).astype(BF)
        received = []
        for k in range(n_adapter):
            piece = lax.dynamic_slice_in_dim(terms, (a ^ k) * half, half, 1)
            received.append(swap(piece, "adapter", n_adapter, k) if k else piece)
        received = jnp.concatenate(received, axis=0)
        place = (
            ((owner ^ a) * owned + slot)[:, None]
            == jnp.arange(n_adapter * owned, dtype=jnp.int32)[None, :]
        ).astype(BF)
        delta = jnp.dot(place, received, preferred_element_type=F32)
        mine = (total + ADAPTER_SCALE * delta).astype(BF)
        other = swap(mine, "tensor", n_tensor, 1)
        return jnp.where(
            low == 0,
            jnp.concatenate([mine, other], axis=1),
            jnp.concatenate([other, mine], axis=1),
        )

    return shards


def solution(mesh):
    in_specs = (
        P(("groups", "adapter"), "tensor"),
        P(("groups", "adapter"), None, "tensor"),
        P(("groups", "adapter"), None, "tensor"),
        P(("groups", "adapter"), "tensor"),
        P(("groups", "adapter"), "tensor"),
        P(("groups", "adapter")),
        P("groups"),
        P(),
        P("tensor", "adapter"),
        P("adapter", "tensor", None),
        P("adapter", "tensor", None),
    )
    out_specs = P("groups", "adapter")
    sizes = mesh.shape["adapter"], mesh.shape["tensor"]
    fast, plain = make_shards(*sizes), make_plain_shards(*sizes)

    def shards(*arrays):
        return (plain if arrays[8].shape[1] % 256 else fast)(*arrays)

    return jax.shard_map(shards, mesh=mesh, in_specs=in_specs, out_specs=out_specs, check_vma=False)
```
